128 devices in a mesh: row: 8 (over y_hi, z), col: 16 (over x, y_lo, core).
Axes of the slice: x: 4, y: 4 (y_hi: 2, y_lo: 2; y = y_hi * 2 + y_lo), z: 4, core: 2. Of those that a mesh axis runs over, the one named last changes fastest.
Arguments:
- object_slab: float32 [2, 4096, 8192], P(None, 'row', 'col'), may hold values from -5 to 5
- probe: float32 [2, 256, 256], replicated, may hold values from -6 to 6
- offsets: int32 [8, 16, 2, 8], P('row', 'col'), may hold values from 0 to 511
- counts: int32 [8, 16], P('row', 'col'), may hold values from 1 to 8, as said below
- patterns: float32 [8, 16, 8, 256, 256], P('row', 'col'), may hold values from 0 to 2
Outputs:
- object_out: float32 [2, 4096, 8192], P(None, 'row', 'col')
- probe_out: float32 [2, 256, 256], replicated
The draws below stay inside these ranges and needn't reach their ends.
Inputs may be any that keep to these rules, and one draw needn't show every extreme that they name: `counts`: some tile has all 8 slots live in every draw.
All inputs are finite; a program needn't handle non-finite values.
Results may differ from the reference program's by a relative error of at most 0.0003.
Values sent between devices are 32-bit elements; how exact they have to be, the bound alone decides.
No kernel may reach another device: no remote copies, remote signals or barrier semaphores. Data moves between devices by JAX's collectives and lax.ppermute only.
A program may use at most 128 MiB of HBM per device.

```python
import jax
import jax.numpy as jnp
from jax import lax

M = 256
TH = 512
TW = 512
SLOT = 8
UPDATES = 2
H = 4096
W = 8192
N_ROW = 8
N_COL = 16


def draw_offsets(key, part):
    key = jax.random.fold_in(key, 11)
    key_rows, key_cols = jax.random.split(key)
    rows_part = jax.random.randint(key_rows, (N_ROW, N_COL, 1, SLOT), 0, TH, dtype=jnp.int32)
    cols_part = jax.random.randint(key_cols, (N_ROW, N_COL, 1, SLOT), 0, TW, dtype=jnp.int32)
    return jnp.concatenate([rows_part, cols_part], axis=2)


def draw_counts(key, part):
    key = jax.random.fold_in(key, 23)
    key_fill, key_pick = jax.random.split(key)
    filled = jax.random.randint(key_fill, (N_ROW * N_COL,), 1, SLOT + 1, dtype=jnp.int32)
    chosen = jax.random.randint(key_pick, (), 0, N_ROW * N_COL, dtype=jnp.int32)
    filled = jnp.where(jnp.arange(N_ROW * N_COL, dtype=jnp.int32) == chosen, SLOT, filled)
    return filled.reshape(N_ROW, N_COL)


def block_levels(own_key, shape, cuts, low, high):
    level = 1.0
    for position, shards_of in cuts:
        heights = jax.random.uniform(jax.random.fold_in(jax.random.fold_in(own_key, 6), position), (shards_of,), jnp.float32, low / len(cuts), high / len(cuts))
        level = level * jnp.repeat(jnp.exp(heights), shape[position] // shards_of).reshape((-1,) + (1,) * (len(shape) - 1 - position))
    return level


def normal_values(rng, shape, spread, most, cuts=(), held_as=jnp.bfloat16):
    values = spread * jax.random.normal(rng, shape, jnp.float32)
    if cuts:
        values = values * block_levels(rng, shape, cuts, -0.22, 0.18)
    return jnp.clip(values, -most, most).astype(held_as)


def setup_inputs(seed: int = 0) -> dict:
    keys = jax.random.split(jax.random.key(seed), 6)
    object_slab = normal_values(keys[0], (2, H, W), 0.7, 5.0, ((1, 8), (2, 16)), jnp.float32)
    probe = normal_values(keys[1], (2, M, M), 1.0, 6.0, (), jnp.float32)
    offsets = draw_offsets(jax.random.fold_in(keys[5], 71), 0)
    counts = draw_counts(jax.random.fold_in(keys[5], 71), 0)
    patterns = jnp.clip(2.0 * jax.random.uniform(keys[4], (N_ROW, N_COL, SLOT, M, M), jnp.float32) ** block_levels(keys[4], (N_ROW, N_COL, SLOT, M, M), ((0, 8), (1, 16)), -0.2, 0.2), 0.0, 2.0)
    return dict(object_slab=object_slab, probe=probe, offsets=offsets, counts=counts, patterns=patterns)


OBJECT_RATE = 0.1
PROBE_RATE = 0.5


def gradients(obj, probe, rows_at, cols_at, live, intens):
    padded = jnp.concatenate([obj, obj[:, :M, :]], axis=1)
    padded = jnp.concatenate([padded, padded[:, :, :M]], axis=2)
    probe_c = probe[0] + 1j * probe[1]
    zero = jnp.zeros((), jnp.int32)

    def step(carry, item):
        grad_pad, grad_probe = carry
        row_y, col_x, alive, inten = item
        patch = lax.dynamic_slice(padded, (zero, row_y.astype(jnp.int32), col_x.astype(jnp.int32)), (2, M, M))
        obj_c = patch[0] + 1j * patch[1]
        wave = jnp.fft.fft2(probe_c * obj_c, norm="ortho")
        resid = (jnp.real(wave) ** 2 + jnp.imag(wave) ** 2 - inten) * alive
        back = jnp.fft.ifft2(resid * wave, norm="ortho")
        go = jnp.conj(probe_c) * back
        gp = jnp.conj(obj_c) * back
        start = (zero, row_y.astype(jnp.int32), col_x.astype(jnp.int32))
        old = lax.dynamic_slice(grad_pad, start, (2, M, M))
        grad_pad = lax.dynamic_update_slice(grad_pad, old + jnp.stack([jnp.real(go), jnp.imag(go)]).astype(grad_pad.dtype), start)
        grad_probe = grad_probe + jnp.stack([jnp.real(gp), jnp.imag(gp)]).astype(grad_probe.dtype)
        return (grad_pad, grad_probe), None

    init = (jnp.zeros(padded.shape, obj.dtype), jnp.zeros(probe.shape, probe.dtype))
    (grad_pad, grad_probe), _ = lax.scan(step, init, (rows_at, cols_at, live, intens))
    height, width = obj.shape[1], obj.shape[2]
    grad_pad = grad_pad.at[:, :, :M].add(grad_pad[:, :, width:])
    grad_pad = grad_pad[:, :, :width]
    grad_pad = grad_pad.at[:, :M, :].add(grad_pad[:, height:, :])
    return grad_pad[:, :height, :], grad_probe


def reference(object_slab, probe, offsets, counts, patterns):
    tile_rows = jnp.arange(N_ROW, dtype=jnp.int32)[:, None, None] * TH
    tile_cols = jnp.arange(N_COL, dtype=jnp.int32)[None, :, None] * TW
    rows_at = (offsets[:, :, 0, :] + tile_rows).reshape(-1)
    cols_at = (offsets[:, :, 1, :] + tile_cols).reshape(-1)
    slot_ids = jnp.arange(SLOT, dtype=jnp.int32)[None, None, :]
    live = (slot_ids < counts[:, :, None]).astype(object_slab.dtype).reshape(-1)
    intens = patterns.reshape(-1, M, M)
    pstep = PROBE_RATE / (N_ROW * N_COL * SLOT) ** 0.5
    obj, prb = object_slab, probe
    for update in range(UPDATES):
        grad_obj, grad_prb = gradients(obj, prb, rows_at, cols_at, live, intens)
        obj = obj - OBJECT_RATE * grad_obj
        prb = prb - pstep * grad_prb
    return obj, prb
```

```python
import math

import jax
import jax.numpy as jnp
import numpy as np
from jax import lax
from jax.experimental import pallas as pl
from jax.experimental.pallas import tpu as pltpu
from jax.sharding import PartitionSpec as P

OBJECT_RATE = 0.1
PROBE_RATE = 0.5
M = 256
HALF = M // 2
LANES = 128
F32 = jnp.float32
BF16 = jnp.bfloat16


def packed_tables():
    j = np.arange(HALF)[:, None]
    k = np.arange(M)[None, :]
    angle = 2.0 * np.pi * ((j * k) % M) / M
    cosine = np.cos(angle)
    sine = np.sin(angle)
    sine[0] = np.where(np.arange(M) % 2 == 0, 1.0, -1.0)
    table = np.concatenate([cosine, sine]) / math.sqrt(M)

    def split(t):
        high = t.astype(jnp.bfloat16)
        low = (t - high.astype(np.float64)).astype(jnp.bfloat16)
        return high, low

    return split(table) + split(table.T)


def split_parts(x):
    high = x.astype(BF16)
    low = (x - high.astype(F32)).astype(BF16)
    return high, low


def mm(a, b):
    return jnp.dot(a, b, preferred_element_type=F32)


def right_mult(x, wh, wl):
    xh, xl = split_parts(x)
    return mm(xh, wh) + (mm(xl, wh) + mm(xh, wl))


def left_mult(wh, wl, x):
    xh, xl = split_parts(x)
    return mm(wh, xh) + (mm(wh, xl) + mm(wl, xh))


def butterfly(uc, us, vc, vs, first):
    rp = uc + jnp.where(first, 0.0, vs)
    rm = jnp.where(first, us, uc - vs)
    ip = vc - jnp.where(first, 0.0, us)
    im = jnp.where(first, vs, vc + us)
    return rp, rm, ip, im


def butterfly_adjoint(rp, rm, ip, im, first):
    uc = rp + jnp.where(first, 0.0, rm)
    vs = jnp.where(first, im, rp - rm)
    vc = ip + jnp.where(first, 0.0, im)
    us = jnp.where(first, rm, im - ip)
    return uc, us, vc, vs


def windows_kernel(offs, count, ext_in, probe, pats, rh, rl, th, tl, gext, gprobe, ext, gacc, pacc):
    for part in range(2):
        for tile in range(6):
            ext[part, tile] = ext_in[part, :, tile * LANES:(tile + 1) * LANES]
    gacc[...] = jnp.zeros(gacc.shape, F32)
    pacc[...] = jnp.zeros(pacc.shape, F32)
    lane = lax.broadcasted_iota(jnp.int32, (M, LANES), 1)
    lane_first = lane == 0
    row_first = lax.broadcasted_iota(jnp.int32, (HALF, M), 0) == 0

    def slot(s, carry):
        r = offs[0, s]
        c = offs[1, s]
        a = c // LANES
        b = c - a * LANES
        rows = pl.ds(r, M)
        keep = lane >= b

        def cut(part):
            t0 = ext[part, a, rows, :]
            t1 = ext[part, a + 1, rows, :]
            t2 = ext[part, a + 2, rows, :]
            return jnp.concatenate([jnp.where(keep, t0, t2), t1], axis=1)

        def turn(part):
            p0 = pltpu.roll(probe[part, :, :LANES], b, 1)
            p1 = pltpu.roll(probe[part, :, LANES:], b, 1)
            return jnp.concatenate([jnp.where(keep, p0, p1), jnp.where(keep, p1, p0)], axis=1)

        o_re, o_im = cut(0), cut(1)
        p_re, p_im = turn(0), turn(1)
        e_re = p_re * o_re - p_im * o_im
        e_im = p_re * o_im + p_im * o_re
        u = left_mult(rh[...], rl[...], right_mult(e_re, th[...], tl[...]))
        v = left_mult(rh[...], rl[...], right_mult(e_im, th[...], tl[...]))
        rp, rm, ip, im = butterfly(u[:, :LANES], u[:, LANES:], v[:, :LANES], v[:, LANES:], lane_first)
        w_re = jnp.concatenate([rp, rm], axis=1)
        w_im = jnp.concatenate([ip, im], axis=1)
        rp, rm, ip, im = butterfly(w_re[:HALF], w_re[HALF:], w_im[:HALF], w_im[HALF:], row_first)
        res_p = rp * rp + ip * ip - pats[s, :HALF]
        res_m = rm * rm + im * im - pats[s, HALF:]
        uc, us, vc, vs = butterfly_adjoint(res_p * rp, res_m * rm, res_p * ip, res_m * im, row_first)
        u = jnp.concatenate([uc, us], axis=0)
        v = jnp.concatenate([vc, vs], axis=0)
        uc, us, vc, vs = butterfly_adjoint(u[:, :LANES], u[:, LANES:], v[:, :LANES], v[:, LANES:], lane_first)
        u = jnp.concatenate([uc, us], axis=1)
        v = jnp.concatenate([vc, vs], axis=1)
        b_re = right_mult(left_mult(th[...], tl[...], u), rh[...], rl[...])
        b_im = right_mult(left_mult(th[...], tl[...], v), rh[...], rl[...])
        go = (p_re * b_re + p_im * b_im, p_re * b_im - p_im * b_re)
        gp = (o_re * b_re + o_im * b_im, o_re * b_im - o_im * b_re)
        back = lane < LANES - b
        for part in range(2):
            g0, g1 = go[part][:, :LANES], go[part][:, LANES:]
            gacc[part, a, rows, :] += jnp.where(keep, g0, 0.0)
            gacc[part, a + 1, rows, :] += g1
            gacc[part, a + 2, rows, :] += jnp.where(keep, 0.0, g0)
            q0 = pltpu.roll(gp[part][:, :LANES], LANES - b, 1)
            q1 = pltpu.roll(gp[part][:, LANES:], LANES - b, 1)
            pacc[part, :, :LANES] += jnp.where(back, q0, q1)
            pacc[part, :, LANES:] += jnp.where(back, q1, q0)
        return carry

    lax.fori_loop(0, count[0], slot, 0)
    for part in range(2):
        for tile in range(6):
            gext[part, :, tile * LANES:(tile + 1) * LANES] = gacc[part, tile]
    gprobe[...] = pacc[...]


def windows(offs, count, ext, probe, pats, tables):
    smem = pl.BlockSpec(memory_space=pltpu.SMEM)
    vmem = pl.BlockSpec(memory_space=pltpu.VMEM)
    side = ext.shape[1]
    tiles = ext.shape[2] // LANES
    return pl.pallas_call(
        windows_kernel,
        out_shape=(jax.ShapeDtypeStruct(ext.shape, F32), jax.ShapeDtypeStruct(probe.shape, F32)),
        in_specs=[smem, smem] + [vmem] * 7,
        out_specs=(vmem, vmem),
        scratch_shapes=[
            pltpu.VMEM((2, tiles, side, LANES), F32),
            pltpu.VMEM((2, tiles, side, LANES), F32),
            pltpu.VMEM(probe.shape, F32),
        ],
        compiler_params=pltpu.CompilerParams(vmem_limit_bytes=56 * 1024 * 1024),
        name="windows",
    )(offs, count, ext, probe, pats, *tables)


def shift(block, axis, distance):
    n = lax.axis_size(axis)
    return lax.ppermute(block, axis, [(i, (i + distance) % n) for i in range(n)])


def sum_everywhere(x, axes):
    n = lax.axis_size(axes)
    parts = x.reshape(n, -1, LANES)
    mine = jnp.sum(lax.all_to_all(parts, axes, 0, 0, tiled=True), axis=0)
    spread = jnp.broadcast_to(mine[None], parts.shape)
    return lax.all_to_all(spread, axes, 0, 0, tiled=True).reshape(x.shape)


def body(object_slab, probe, offsets, counts, patterns):
    tile_h, tile_w = object_slab.shape[1:]
    slots = patterns.shape[2]
    offs = offsets[0, 0]
    count = counts[0]
    tables = tuple(jnp.asarray(t) for t in packed_tables())
    axes = ("row", "col")
    pstep = PROBE_RATE / math.sqrt(lax.axis_size(axes) * slots)

    pats = patterns[0, 0]
    order = np.concatenate([np.arange(HALF + 1), np.arange(M - 1, HALF, -1)])
    turned = np.zeros((M, M), np.float32)
    turned[np.arange(M), order] = 1.0
    high = lax.Precision.HIGHEST
    pats = jnp.einsum("jk,skl->sjl", turned, pats, precision=high)
    pats = jnp.einsum("sjk,lk->sjl", pats, turned, precision=high)

    below = shift(object_slab[:, :M, :], "row", -1)
    taller = jnp.concatenate([object_slab, below], axis=1)
    beside = shift(taller[:, :, :M], "col", -1)
    ext = jnp.concatenate([taller, beside], axis=2)

    gext, gprobe = windows(offs, count, ext, probe, pats, tables)
    from_above = shift(gext[:, tile_h:], "row", 1)
    from_below = shift(gext[:, :M], "row", -1)
    gext = gext.at[:, :M].add(from_above).at[:, tile_h:].add(from_below)
    from_left = shift(gext[:, :, tile_w:], "col", 1)
    from_right = shift(gext[:, :, :M], "col", -1)
    gext = gext.at[:, :, :M].add(from_left).at[:, :, tile_w:].add(from_right)
    ext = ext - OBJECT_RATE * gext
    probe = probe - pstep * sum_everywhere(gprobe, axes)

    gext, gprobe = windows(offs, count, ext, probe, pats, tables)
    from_above = shift(gext[:, tile_h:], "row", 1)
    upper = gext[:, :tile_h].at[:, :M].add(from_above)
    from_left = shift(upper[:, :, tile_w:], "col", 1)
    grad = upper[:, :, :tile_w].at[:, :, :M].add(from_left)
    probe = probe - pstep * sum_everywhere(gprobe, axes)
    return ext[:, :tile_h, :tile_w] - OBJECT_RATE * grad, probe


def solution(mesh):
    placed = (
        P(None, "row", "col"),
        P(),
        P("row", "col", None, None),
        P("row", "col"),
        P("row", "col", None, None, None),
    )
    return jax.shard_map(
        body, mesh=mesh, in_specs=placed, out_specs=(P(None, "row", "col"), P()), check_vma=False
    )
```

```python
import functools
import itertools
import math

import jax
import jax.numpy as jnp
import numpy as np
from jax import lax
from jax.experimental import pallas as pl
from jax.experimental.pallas import tpu as pltpu
from jax.sharding import Mesh, PartitionSpec as P

OBJECT_RATE = 0.1
PROBE_RATE = 0.5
M = 256
HALF = M // 2
LANES = 128
COL = ("x", "y_lo", "core")
STRIP = 32
F32 = jnp.float32
BF16 = jnp.bfloat16


def packed_tables():
    j = np.arange(HALF)[:, None]
    k = np.arange(M)[None, :]
    angle = 2.0 * np.pi * ((j * k) % M) / M
    cosine = np.cos(angle)
    sine = np.sin(angle)
    sine[0] = np.where(np.arange(M) % 2 == 0, 1.0, -1.0)
    table = np.concatenate([cosine, sine]) / math.sqrt(M)

    def split(t):
        high = t.astype(jnp.bfloat16)
        low = (t - high.astype(np.float64)).astype(jnp.bfloat16)
        return high, low

    return split(table) + split(table.T)


def split_parts(x):
    high = x.astype(BF16)
    low = (x - high.astype(F32)).astype(BF16)
    return high, low

def butterfly(uc, us, vc, vs, first):
    if first is None:
        return uc + vs, uc - vs, vc - us, vc + us
    rp = uc + jnp.where(first, 0.0, vs)
    rm = jnp.where(first, us, uc - vs)
    ip = vc - jnp.where(first, 0.0, us)
    im = jnp.where(first, vs, vc + us)
    return rp, rm, ip, im

def butterfly_adjoint(rp, rm, ip, im, first):
    if first is None:
        return rp + rm, im - ip, ip + im, rp - rm
    uc = rp + jnp.where(first, 0.0, rm)
    vs = jnp.where(first, im, rp - rm)
    vc = ip + jnp.where(first, 0.0, im)
    us = jnp.where(first, rm, im - ip)
    return uc, us, vc, vs

def halves(x):
    return x[:, :LANES], x[:, LANES:]

def window(s, live, offs, probe, pats, tables, ext, gacc, pacc, scratch):
    rh, rl, th, tl = tables
    ah, al, bh, bl, f, pr = scratch
    r = offs[0, s]
    c = offs[1, s]
    a = c // LANES
    b = c - a * LANES
    lane = lax.broadcasted_iota(jnp.int32, (STRIP, LANES), 1)
    keep = lane >= b
    lane_first = lane == 0
    row_first = lax.broadcasted_iota(jnp.int32, (STRIP, M), 0) == 0

    def cut(part, i):
        rows = pl.ds(r + i * STRIP, STRIP)
        t0 = ext[a, part, rows, :]
        t1 = ext[a + 1, part, rows, :]
        t2 = ext[a + 2, part, rows, :]
        return jnp.concatenate([jnp.where(keep, t0, t2), t1], axis=1)

    def turn(part, i):
        rows = pl.ds(i * STRIP, STRIP)
        p0 = pltpu.roll(probe[0, part, rows, :], b, 1)
        p1 = pltpu.roll(probe[1, part, rows, :], b, 1)
        return jnp.concatenate([jnp.where(keep, p0, p1), jnp.where(keep, p1, p0)], axis=1)

    def put(high, low, part, rows, value):
        h, l = split_parts(value)
        high[part, rows, :] = h
        low[part, rows, :] = l

    def right(high, low, wh, wl, emit):
        w = jnp.concatenate([wh[...], wh[...], wl[...]], axis=0)
        for part in range(2):
            h, l = high[part], low[part]
            emit(part, slice(0, M), jnp.dot(jnp.concatenate([h, l, h], axis=1), w, preferred_element_type=F32))

    def left(wh, wl, high, low, emit):
        w = jnp.concatenate([wh[...], wl[...], wh[...]], axis=1)
        for part in range(2):
            h, l = high[part], low[part]
            x = jnp.concatenate([h, h, l], axis=0)
            emit(part, slice(0, M), jnp.dot(w, x, preferred_element_type=F32))

    def keep_f32(part, rows, value):
        f[part, rows, :] = value

    for i in range(M // STRIP):
        rows = slice(i * STRIP, (i + 1) * STRIP)
        o_re, o_im = cut(0, i), cut(1, i)
        p_re, p_im = turn(0, i), turn(1, i)
        pr[0, rows, :] = p_re
        pr[1, rows, :] = p_im
        put(ah, al, 0, rows, p_re * o_re - p_im * o_im)
        put(ah, al, 1, rows, p_re * o_im + p_im * o_re)
    yield
    right(ah, al, th, tl, functools.partial(put, bh, bl))
    yield
    left(rh, rl, bh, bl, keep_f32)
    yield
    for i in range(HALF // STRIP):
        top = slice(i * STRIP, (i + 1) * STRIP)
        bot = slice(HALF + i * STRIP, HALF + (i + 1) * STRIP)
        first = row_first if i == 0 else None
        u_c, u_s, v_c, v_s = f[0, top, :], f[0, bot, :], f[1, top, :], f[1, bot, :]
        wide = []
        for u, v in ((u_c, v_c), (u_s, v_s)):
            rp, rm, ip, im = butterfly(*halves(u), *halves(v), lane_first)
            wide += [jnp.concatenate([rp, rm], axis=1), jnp.concatenate([ip, im], axis=1)]
        rp, rm, ip, im = butterfly(wide[0], wide[2], wide[1], wide[3], first)
        res_p = rp * rp + ip * ip - pats[s, top, :]
        res_m = rm * rm + im * im - pats[s, bot, :]
        if live is not None:
            res_p, res_m = res_p * live, res_m * live
        uc, us, vc, vs = butterfly_adjoint(res_p * rp, res_m * rm, res_p * ip, res_m * im, first)
        for u, v, rows in ((uc, vc, top), (us, vs, bot)):
            x_c, x_s, y_c, y_s = butterfly_adjoint(*halves(u), *halves(v), lane_first)
            put(ah, al, 0, rows, jnp.concatenate([x_c, x_s], axis=1))
            put(ah, al, 1, rows, jnp.concatenate([y_c, y_s], axis=1))
    yield
    left(th, tl, ah, al, functools.partial(put, bh, bl))
    yield
    right(bh, bl, rh, rl, keep_f32)
    yield
    back = lane < LANES - b
    for i in range(M // STRIP):
        rows = slice(i * STRIP, (i + 1) * STRIP)
        spot = pl.ds(r + i * STRIP, STRIP)
        b_re, b_im = f[0, rows, :], f[1, rows, :]
        o_re, o_im = cut(0, i), cut(1, i)
        p_re, p_im = pr[0, rows, :], pr[1, rows, :]
        go = (p_re * b_re + p_im * b_im, p_re * b_im - p_im * b_re)
        gp = (o_re * b_re + o_im * b_im, o_re * b_im - o_im * b_re)
        for part in range(2):
            g0, g1 = halves(go[part])
            gacc[a, part, spot, :] += jnp.where(keep, g0, 0.0)
            gacc[a + 1, part, spot, :] += g1
            gacc[a + 2, part, spot, :] += jnp.where(keep, 0.0, g0)
            q0, q1 = halves(gp[part])
            q0 = pltpu.roll(q0, LANES - b, 1)
            q1 = pltpu.roll(q1, LANES - b, 1)
            pacc[0, part, rows, :] += jnp.where(back, q0, q1)
            pacc[1, part, rows, :] += jnp.where(back, q1, q0)


def windows_kernel(*refs):
    offs, count = refs[:2]
    blocks, (probe, pats) = refs[2:11], refs[11:13]
    tables, grads, gprobe = refs[13:17], refs[17:26], refs[26]
    ext, gacc, pats_here, *scratch, sem_in, sem_out, sem_pats = refs[27:]

    def place(buffer, k):
        i, j = divmod(k, 3)
        return buffer.at[2 * j:2 * j + 2, :, i * M:(i + 1) * M, :]

    arrivals = [pltpu.make_async_copy(blocks[k], place(ext, k), sem_in.at[k]) for k in range(9)]
    arrivals.append(pltpu.make_async_copy(pats, pats_here, sem_pats))
    for copy in arrivals:
        copy.start()

    def clear(i, carry):
        gacc[:, :, pl.ds(i * STRIP, STRIP), :] = jnp.zeros((6, 2, STRIP, LANES), F32)
        return carry

    lax.fori_loop(0, 3 * M // STRIP, clear, 0)
    gprobe[...] = jnp.zeros(gprobe.shape, F32)
    for copy in arrivals:
        copy.wait()

    def pair(k, carry):
        turns = []
        for n in range(2):
            live = None if n == 0 else jnp.where(2 * k + 1 < count[0], 1.0, 0.0)
            own = [buffer.at[n] for buffer in scratch]
            turns.append(window(2 * k + n, live, offs, probe, pats_here, tables, ext, gacc, gprobe, own))
        for _ in itertools.zip_longest(*turns):
            pass
        return carry

    lax.fori_loop(0, (count[0] + 1) // 2, pair, 0)
    departures = [pltpu.make_async_copy(place(gacc, k), grads[k], sem_out.at[k]) for k in range(9)]
    for copy in departures:
        copy.start()
    for copy in departures:
        copy.wait()


def in_hbm(arrays):
    return [pltpu.with_memory_space_constraint(x, pltpu.HBM) for x in arrays]


def windows(offs, count, blocks, probe, pats, tables):
    smem = pl.BlockSpec(memory_space=pltpu.SMEM)
    vmem = pl.BlockSpec(memory_space=pltpu.VMEM)
    where = pl.BlockSpec(memory_space=pl.ANY)
    block = jax.ShapeDtypeStruct((2, 2, M, LANES), F32)
    halves16 = pltpu.VMEM((2, 2, M, M), BF16)
    whole32 = pltpu.VMEM((2, 2, M, M), F32)
    extended = pltpu.VMEM((6, 2, 3 * M, LANES), F32)
    return pl.pallas_call(
        windows_kernel,
        out_shape=[pltpu.HBM(block.shape, F32)] * 9 + [block],
        in_specs=[smem, smem] + [where] * 9 + [vmem, where] + [vmem] * 4,
        out_specs=[where] * 9 + [vmem],
        scratch_shapes=[extended, extended, pltpu.VMEM(pats.shape, F32)] + [halves16] * 4 + [whole32] * 2
        + [pltpu.SemaphoreType.DMA((9,)), pltpu.SemaphoreType.DMA((9,)), pltpu.SemaphoreType.DMA],
        compiler_params=pltpu.CompilerParams(vmem_limit_bytes=24 * 1024 * 1024),
        name="windows",
    )(offs, count, *in_hbm(blocks), probe, *in_hbm([pats]), *tables)


def shift(block, axis, distance):
    n = lax.axis_size(axis)
    return lax.ppermute(block, axis, [(i, (i + distance) % n) for i in range(n)])


RING = 4


def shift_z(block, distance):
    pairs = [(i, i // RING * RING + (i + distance) % RING) for i in range(lax.axis_size("row"))]
    return lax.ppermute(block, "row", pairs)


def cross_y(block, distance):
    n, edge = lax.axis_size("row"), 0 if distance > 0 else RING - 1
    far = lax.ppermute(block, "row", [(i, (i + RING) % n) for i in range(edge, n, RING)])
    return jnp.where(lax.axis_index("row") % RING == edge, far, block)


def most_kernel(*refs):
    whole, here, sem = refs[11:]
    arrivals = [pltpu.make_async_copy(refs[k], here.at[k], sem.at[k]) for k in range(11)]
    for copy in arrivals:
        copy.start()
    for copy in arrivals:
        copy.wait()
    for k, grads in enumerate(((4, 8), (5, 9), (6, 10), (7,))):
        i, j = divmod(k, 2)
        for tile in range(2):
            lanes = pl.ds((2 * j + tile) * LANES, LANES)
            for part in range(2):
                total = sum((here[g, tile, part] for g in grads[1:]), here[grads[0], tile, part])
                whole[part, pl.ds(i * M, M), lanes] = here[k, tile, part] - OBJECT_RATE * total


def rest_kernel(pstep, grad, probe, summed, whole_in, whole, probe_out, corner, sem):
    del whole_in
    view = whole.at[:, pl.ds(0, M), pl.ds(0, M)]
    arrive = pltpu.make_async_copy(view, corner, sem.at[0])
    arrive.start()
    for tile in range(2):
        for part in range(2):
            lanes = pl.ds(tile * LANES, LANES)
            probe_out[part, :, lanes] = probe[tile, part] - pstep * summed[tile, part]
    arrive.wait()
    for tile in range(2):
        for part in range(2):
            lanes = pl.ds(tile * LANES, LANES)
            corner[part, :, lanes] = corner[part, :, lanes] - OBJECT_RATE * grad[tile, part]
    leave = pltpu.make_async_copy(corner, view, sem.at[1])
    leave.start()
    leave.wait()


def most(own, grads):
    vmem, where = pl.BlockSpec(memory_space=pltpu.VMEM), pl.BlockSpec(memory_space=pl.ANY)
    return pl.pallas_call(
        most_kernel,
        out_shape=jax.ShapeDtypeStruct((2, 2 * M, 2 * M), F32),
        in_specs=[where] * 11,
        out_specs=vmem,
        scratch_shapes=[pltpu.VMEM((11, *own[0].shape), F32), pltpu.SemaphoreType.DMA((11,))],
        compiler_params=pltpu.CompilerParams(vmem_limit_bytes=24 * 1024 * 1024),
        name="most",
    )(*in_hbm([*own, *grads]))


def rest(pstep, grad, probe, summed, whole):
    vmem, where = pl.BlockSpec(memory_space=pltpu.VMEM), pl.BlockSpec(memory_space=pl.ANY)
    return pl.pallas_call(
        functools.partial(rest_kernel, pstep),
        out_shape=(pltpu.HBM(whole.shape, F32), jax.ShapeDtypeStruct((2, M, M), F32)),
        in_specs=[vmem] * 3 + [where],
        out_specs=(where, vmem),
        scratch_shapes=[pltpu.VMEM((2, M, M), F32), pltpu.SemaphoreType.DMA((2,))],
        input_output_aliases={3: 0},
        compiler_params=pltpu.CompilerParams(vmem_limit_bytes=24 * 1024 * 1024),
        name="rest",
    )(grad, probe, summed, *in_hbm([whole]))


def deal(x):
    return jnp.sum(lax.all_to_all(x.reshape(-1, 8, LANES), ("row", *COL), 0, 0, tiled=True), axis=0)


def collect(share, shape):
    n = lax.axis_size(("row", *COL))
    spread = jnp.broadcast_to(share[None], (n, *share.shape))
    return lax.all_to_all(spread, ("row", *COL), 0, 0, tiled=True).reshape(shape)


def together(*values):
    return lax.optimization_barrier(values)


def tile_block(x, i, j):
    part = x[:, i * M:(i + 1) * M, j * M:(j + 1) * M]
    return jnp.stack([part[:, :, :LANES], part[:, :, LANES:]])


def body(object_slab, probe, offsets, counts, patterns):
    tile_h, tile_w = object_slab.shape[1:]
    slots = patterns.shape[2]
    offs = offsets[0, 0]
    count = counts[0]
    tables = tuple(jnp.asarray(t) for t in packed_tables())
    axes = ("row", *COL)
    pstep = PROBE_RATE / math.sqrt(lax.axis_size(axes) * slots)

    pats = patterns[0, 0]
    order = np.concatenate([np.arange(HALF + 1), np.arange(M - 1, HALF, -1)])
    turned = np.zeros((M, M), np.float32)
    turned[np.arange(M), order] = 1.0
    high = lax.Precision.HIGHEST
    pats = jnp.einsum("jk,skl->sjl", turned, pats, precision=high)
    pats = jnp.einsum("sjk,lk->sjl", pats, turned, precision=high)

    def step(x, *grads):
        return x - OBJECT_RATE * sum(grads[1:], grads[0])

    probe = tile_block(probe, 0, 0)
    own00, own01 = tile_block(object_slab, 0, 0), tile_block(object_slab, 0, 1)
    own10, own11 = tile_block(object_slab, 1, 0), tile_block(object_slab, 1, 1)
    own20, own21 = shift(own00, "row", -1), shift(own01, "row", -1)
    own02, own12 = shift(own00, COL, -1), shift(own10, COL, -1)
    own22 = shift(own20, COL, -1)

    blocks = (own00, own01, own02, own10, own11, own12, own20, own21, own22)
    g00, g01, g02, g10, g11, g12, g20, g21, g22, gprobe = windows(offs, count, blocks, probe, pats, tables)
    left0, left2, above1, under1, share = together(
        shift(g02, COL, 1), shift(g22, COL, 1), shift(g21, "row", 1), shift(g01, "row", -1), deal(gprobe)
    )
    g00, g20, share = together(g00 + left0, g20 + left2, share)
    above0, under0, left1, own01, own11, own21 = together(
        shift(g20, "row", 1), shift(g00, "row", -1), shift(g12, COL, 1),
        step(own01, g01, above1), step(own11, g11), step(own21, g21, under1),
    )
    own00, own20, own10, share = together(
        step(own00, g00, above0), step(own20, g20, under0), step(own10, g10, left1), share
    )
    own02, own22, own12, summed = together(
        shift(own00, COL, -1), shift(own20, COL, -1), shift(own10, COL, -1), collect(share, probe.shape)
    )
    probe = probe - pstep * summed

    blocks = (own00, own01, own02, own10, own11, own12, own20, own21, own22)
    g00, g01, g02, g10, g11, g12, g20, g21, g22, gprobe = windows(offs, count, blocks, probe, pats, tables)
    left2, left0, left1, above1, share = together(
        shift(g22, COL, 1), shift(g02, COL, 1), shift(g12, COL, 1), shift_z(g21, 1), deal(gprobe)
    )
    g20, share = together(g20 + left2, share)
    whole = most((own00, own01, own10, own11), (g00, g01, g10, g11, left0, cross_y(above1, 1), left1))
    above0, summed, whole = together(shift(g20, "row", 1), collect(share, probe.shape), whole)
    return rest(pstep, above0, probe, summed, whole)


def solution(mesh):
    mesh = Mesh(mesh.devices.reshape(-1, 4, 2, 2), ("row", *COL))
    placed = (
        P(None, "row", COL),
        P(),
        P("row", COL, None, None),
        P("row", COL),
        P("row", COL, None, None, None),
    )
    return jax.shard_map(
        body, mesh=mesh, in_specs=placed, out_specs=(P(None, "row", COL), P()), check_vma=False
    )
```

```python
import functools
import itertools
import math

import jax
import jax.numpy as jnp
import numpy as np
from jax import lax
from jax.experimental import pallas as pl
from jax.experimental.pallas import tpu as pltpu
from jax.sharding import Mesh, PartitionSpec as P

OBJECT_RATE = 0.1
PROBE_RATE = 0.5
M = 256
HALF = M // 2
LANES = 128
COL = ("x", "y_lo", "core")
STRIP = 32
F32 = jnp.float32
BF16 = jnp.bfloat16


def packed_tables():
    j = np.arange(HALF)[:, None]
    k = np.arange(M)[None, :]
    angle = 2.0 * np.pi * ((j * k) % M) / M
    cosine = np.cos(angle)
    sine = np.sin(angle)
    sine[0] = np.where(np.arange(M) % 2 == 0, 1.0, -1.0)
    table = np.concatenate([cosine, sine]) / math.sqrt(M)

    def split(t):
        high = t.astype(jnp.bfloat16)
        low = (t - high.astype(np.float64)).astype(jnp.bfloat16)
        return high, low

    return split(table) + split(table.T)


def split_parts(x):
    high = x.astype(BF16)
    low = (x - high.astype(F32)).astype(BF16)
    return high, low

def butterfly(uc, us, vc, vs, first):
    if first is None:
        return uc + vs, uc - vs, vc - us, vc + us
    rp = uc + jnp.where(first, 0.0, vs)
    rm = jnp.where(first, us, uc - vs)
    ip = vc - jnp.where(first, 0.0, us)
    im = jnp.where(first, vs, vc + us)
    return rp, rm, ip, im

def butterfly_adjoint(rp, rm, ip, im, first):
    if first is None:
        return rp + rm, im - ip, ip + im, rp - rm
    uc = rp + jnp.where(first, 0.0, rm)
    vs = jnp.where(first, im, rp - rm)
    vc = ip + jnp.where(first, 0.0, im)
    us = jnp.where(first, rm, im - ip)
    return uc, us, vc, vs

def halves(x):
    return x[:, :LANES], x[:, LANES:]

def window(s, live, offs, probe, pats, tables, ext, gacc, pacc, scratch):
    rh, rl, th, tl = tables
    ah, al, bh, bl, f, pr = scratch
    r = offs[0, s]
    c = offs[1, s]
    a = c // LANES
    b = c - a * LANES
    lane = lax.broadcasted_iota(jnp.int32, (STRIP, LANES), 1)
    keep = lane >= b
    lane_first = lane == 0
    row_first = lax.broadcasted_iota(jnp.int32, (STRIP, M), 0) == 0

    def cut(part, i):
        rows = pl.ds(r + i * STRIP, STRIP)
        t0 = ext[a, part, rows, :]
        t1 = ext[a + 1, part, rows, :]
        t2 = ext[a + 2, part, rows, :]
        return jnp.concatenate([jnp.where(keep, t0, t2), t1], axis=1)

    def turn(part, i):
        rows = pl.ds(i * STRIP, STRIP)
        p0 = pltpu.roll(probe[0, part, rows, :], b, 1)
        p1 = pltpu.roll(probe[1, part, rows, :], b, 1)
        return jnp.concatenate([jnp.where(keep, p0, p1), jnp.where(keep, p1, p0)], axis=1)

    def put(high, low, part, rows, value):
        h, l = split_parts(value)
        high[part, rows, :] = h
        low[part, rows, :] = l

    def right(high, low, wh, wl, emit):
        w = jnp.concatenate([wh[...], wh[...], wl[...]], axis=0)
        for part in range(2):
            h, l = high[part], low[part]
            emit(part, slice(0, M), jnp.dot(jnp.concatenate([h, l, h], axis=1), w, preferred_element_type=F32))

    def left(wh, wl, high, low, emit):
        w = jnp.concatenate([wh[...], wl[...], wh[...]], axis=1)
        for part in range(2):
            h, l = high[part], low[part]
            x = jnp.concatenate([h, h, l], axis=0)
            emit(part, slice(0, M), jnp.dot(w, x, preferred_element_type=F32))

    def keep_f32(part, rows, value):
        f[part, rows, :] = value

    for i in range(M // STRIP):
        rows = slice(i * STRIP, (i + 1) * STRIP)
        o_re, o_im = cut(0, i), cut(1, i)
        p_re, p_im = turn(0, i), turn(1, i)
        pr[0, rows, :] = p_re
        pr[1, rows, :] = p_im
        put(ah, al, 0, rows, p_re * o_re - p_im * o_im)
        put(ah, al, 1, rows, p_re * o_im + p_im * o_re)
    yield
    right(ah, al, th, tl, functools.partial(put, bh, bl))
    yield
    left(rh, rl, bh, bl, keep_f32)
    yield
    for i in range(HALF // STRIP):
        top = slice(i * STRIP, (i + 1) * STRIP)
        bot = slice(HALF + i * STRIP, HALF + (i + 1) * STRIP)
        first = row_first if i == 0 else None
        u_c, u_s, v_c, v_s = f[0, top, :], f[0, bot, :], f[1, top, :], f[1, bot, :]
        wide = []
        for u, v in ((u_c, v_c), (u_s, v_s)):
            rp, rm, ip, im = butterfly(*halves(u), *halves(v), lane_first)
            wide += [jnp.concatenate([rp, rm], axis=1), jnp.concatenate([ip, im], axis=1)]
        rp, rm, ip, im = butterfly(wide[0], wide[2], wide[1], wide[3], first)
        res_p = rp * rp + ip * ip - pats[s, top, :]
        res_m = rm * rm + im * im - pats[s, bot, :]
        if live is not None:
            res_p, res_m = res_p * live, res_m * live
        uc, us, vc, vs = butterfly_adjoint(res_p * rp, res_m * rm, res_p * ip, res_m * im, first)
        for u, v, rows in ((uc, vc, top), (us, vs, bot)):
            x_c, x_s, y_c, y_s = butterfly_adjoint(*halves(u), *halves(v), lane_first)
            put(ah, al, 0, rows, jnp.concatenate([x_c, x_s], axis=1))
            put(ah, al, 1, rows, jnp.concatenate([y_c, y_s], axis=1))
    yield
    left(th, tl, ah, al, functools.partial(put, bh, bl))
    yield
    right(bh, bl, rh, rl, keep_f32)
    yield
    back = lane < LANES - b
    for i in range(M // STRIP):
        rows = slice(i * STRIP, (i + 1) * STRIP)
        spot = pl.ds(r + i * STRIP, STRIP)
        b_re, b_im = f[0, rows, :], f[1, rows, :]
        o_re, o_im = cut(0, i), cut(1, i)
        p_re, p_im = pr[0, rows, :], pr[1, rows, :]
        go = (p_re * b_re + p_im * b_im, p_re * b_im - p_im * b_re)
        gp = (o_re * b_re + o_im * b_im, o_re * b_im - o_im * b_re)
        for part in range(2):
            g0, g1 = halves(go[part])
            gacc[a, part, spot, :] += jnp.where(keep, g0, 0.0)
            gacc[a + 1, part, spot, :] += g1
            gacc[a + 2, part, spot, :] += jnp.where(keep, 0.0, g0)
            q0, q1 = halves(gp[part])
            q0 = pltpu.roll(q0, LANES - b, 1)
            q1 = pltpu.roll(q1, LANES - b, 1)
            pacc[0, part, rows, :] += jnp.where(back, q0, q1)
            pacc[1, part, rows, :] += jnp.where(back, q1, q0)


def windows_kernel(*refs):
    offs, count = refs[:2]
    blocks, (probe, pats) = refs[2:11], refs[11:13]
    tables, grads, gprobe = refs[13:17], refs[17:26], refs[26]
    ext, gacc, pats_here, *scratch, sem_in, sem_out, sem_pats = refs[27:]

    def place(buffer, k):
        i, j = divmod(k, 3)
        return buffer.at[2 * j:2 * j + 2, :, i * M:(i + 1) * M, :]

    arrivals = [pltpu.make_async_copy(blocks[k], place(ext, k), sem_in.at[k]) for k in range(9)]
    arrivals.append(pltpu.make_async_copy(pats, pats_here, sem_pats))
    for copy in arrivals:
        copy.start()

    def clear(i, carry):
        gacc[:, :, pl.ds(i * STRIP, STRIP), :] = jnp.zeros((6, 2, STRIP, LANES), F32)
        return carry

    lax.fori_loop(0, 3 * M // STRIP, clear, 0)
    gprobe[...] = jnp.zeros(gprobe.shape, F32)
    for copy in arrivals:
        copy.wait()

    def pair(k, carry):
        turns = []
        for n in range(4):
            live = None if n == 0 else jnp.where(4 * k + n < count[0], 1.0, 0.0)
            own = [buffer.at[n] for buffer in scratch]
            turns.append(window(4 * k + n, live, offs, probe, pats_here, tables, ext, gacc, gprobe, own))
        for _ in itertools.zip_longest(*turns):
            pass
        return carry

    lax.fori_loop(0, (count[0] + 3) // 4, pair, 0)
    departures = [pltpu.make_async_copy(place(gacc, k), grads[k], sem_out.at[k]) for k in range(9)]
    for copy in departures:
        copy.start()
    for copy in departures:
        copy.wait()


def in_hbm(arrays):
    return [pltpu.with_memory_space_constraint(x, pltpu.HBM) for x in arrays]


def windows(offs, count, blocks, probe, pats, tables):
    smem = pl.BlockSpec(memory_space=pltpu.SMEM)
    vmem = pl.BlockSpec(memory_space=pltpu.VMEM)
    where = pl.BlockSpec(memory_space=pl.ANY)
    block = jax.ShapeDtypeStruct((2, 2, M, LANES), F32)
    halves16 = pltpu.VMEM((4, 2, M, M), BF16)
    whole32 = pltpu.VMEM((4, 2, M, M), F32)
    extended = pltpu.VMEM((6, 2, 3 * M, LANES), F32)
    return pl.pallas_call(
        windows_kernel,
        out_shape=[pltpu.HBM(block.shape, F32)] * 9 + [block],
        in_specs=[smem, smem] + [where] * 9 + [vmem, where] + [vmem] * 4,
        out_specs=[where] * 9 + [vmem],
        scratch_shapes=[extended, extended, pltpu.VMEM(pats.shape, F32)] + [halves16] * 4 + [whole32] * 2
        + [pltpu.SemaphoreType.DMA((9,)), pltpu.SemaphoreType.DMA((9,)), pltpu.SemaphoreType.DMA],
        compiler_params=pltpu.CompilerParams(vmem_limit_bytes=34 * 1024 * 1024),
        name="windows",
    )(offs, count, *in_hbm(blocks), probe, *in_hbm([pats]), *tables)


def shift(block, axis, distance):
    n = lax.axis_size(axis)
    return lax.ppermute(block, axis, [(i, (i + distance) % n) for i in range(n)])


RING = 4


def shift_z(block, distance):
    pairs = [(i, i // RING * RING + (i + distance) % RING) for i in range(lax.axis_size("row"))]
    return lax.ppermute(block, "row", pairs)


def cross_y(block, distance):
    n, edge = lax.axis_size("row"), 0 if distance > 0 else RING - 1
    wrapped = (lax.axis_index("row") % RING == edge).astype(jnp.int32).reshape(1)
    return lax.ppermute(block, "row", [(i, (i + RING) % n) for i in range(edge, n, RING)]), wrapped


def fetch(refs, here, sem):
    copies = [pltpu.make_async_copy(ref, here.at[k], sem.at[k]) for k, ref in enumerate(refs)]
    for copy in copies:
        copy.start()
    for copy in copies:
        copy.wait()


def most_kernel(*refs):
    whole, here, sem = refs[10:]
    fetch(refs[:10], here, sem)
    for k, grads in enumerate(((4, 8), (5,), (6, 9), (7,))):
        i, j = divmod(k, 2)
        for tile in range(2):
            lanes = pl.ds((2 * j + tile) * LANES, LANES)
            for part in range(2):
                total = sum((here[g, tile, part] for g in grads[1:]), here[grads[0], tile, part])
                whole[part, pl.ds(i * M, M), lanes] = here[k, tile, part] - OBJECT_RATE * total


def rest_kernel(pstep, wrapped, above0, near, far, probe, summed, whole_in, whole, probe_out, top, here, sem, sem_top):
    del whole_in
    view = whole.at[:, pl.ds(0, M), :]
    arrive = pltpu.make_async_copy(view, top, sem_top.at[0])
    arrive.start()
    fetch((above0, near, far, probe, summed), here, sem)
    arrive.wait()
    from_far = wrapped[0] == 1
    for tile in range(2):
        for part in range(2):
            lanes, beside = pl.ds(tile * LANES, LANES), pl.ds((2 + tile) * LANES, LANES)
            top[part, :, lanes] = top[part, :, lanes] - OBJECT_RATE * here[0, tile, part]
            above1 = jnp.where(from_far, here[2, tile, part], here[1, tile, part])
            top[part, :, beside] = top[part, :, beside] - OBJECT_RATE * above1
    leave = pltpu.make_async_copy(top, view, sem_top.at[1])
    leave.start()
    for tile in range(2):
        for part in range(2):
            lanes = pl.ds(tile * LANES, LANES)
            probe_out[part, :, lanes] = here[3, tile, part] - pstep * here[4, tile, part]
    leave.wait()


def most(own, grads):
    vmem, where = pl.BlockSpec(memory_space=pltpu.VMEM), pl.BlockSpec(memory_space=pl.ANY)
    return pl.pallas_call(
        most_kernel,
        out_shape=jax.ShapeDtypeStruct((2, 2 * M, 2 * M), F32),
        in_specs=[where] * 10,
        out_specs=vmem,
        scratch_shapes=[pltpu.VMEM((10, *own[0].shape), F32), pltpu.SemaphoreType.DMA((10,))],
        compiler_params=pltpu.CompilerParams(vmem_limit_bytes=24 * 1024 * 1024),
        name="most",
    )(*in_hbm([*own, *grads]))


def rest(pstep, wrapped, moved, probe, summed, whole):
    smem, vmem = pl.BlockSpec(memory_space=pltpu.SMEM), pl.BlockSpec(memory_space=pltpu.VMEM)
    where = pl.BlockSpec(memory_space=pl.ANY)
    return pl.pallas_call(
        functools.partial(rest_kernel, pstep),
        out_shape=(pltpu.HBM(whole.shape, F32), jax.ShapeDtypeStruct((2, M, M), F32)),
        in_specs=[smem] + [where] * 6,
        out_specs=(where, vmem),
        scratch_shapes=[
            pltpu.VMEM((2, M, 2 * M), F32),
            pltpu.VMEM((5, *probe.shape), F32),
            pltpu.SemaphoreType.DMA((5,)),
            pltpu.SemaphoreType.DMA((2,)),
        ],
        input_output_aliases={6: 0},
        compiler_params=pltpu.CompilerParams(vmem_limit_bytes=24 * 1024 * 1024),
        name="rest",
    )(wrapped, *in_hbm([*moved, probe, summed, whole]))


def deal(x):
    return lax.all_to_all(x.reshape(-1, 8, LANES), ("row", *COL), 0, 0, tiled=True)


def collect(terms, shape):
    spread = jnp.broadcast_to(jnp.sum(terms, axis=0)[None], terms.shape)
    return lax.all_to_all(spread, ("row", *COL), 0, 0, tiled=True).reshape(shape)


def together(*values):
    return lax.optimization_barrier(values)


def tile_block(x, i, j):
    part = x[:, i * M:(i + 1) * M, j * M:(j + 1) * M]
    return jnp.stack([part[:, :, :LANES], part[:, :, LANES:]])


def body(object_slab, probe, offsets, counts, patterns):
    tile_h, tile_w = object_slab.shape[1:]
    slots = patterns.shape[2]
    offs = offsets[0, 0]
    count = counts[0]
    tables = tuple(jnp.asarray(t) for t in packed_tables())
    axes = ("row", *COL)
    pstep = PROBE_RATE / math.sqrt(lax.axis_size(axes) * slots)

    pats = patterns[0, 0]
    order = np.concatenate([np.arange(HALF + 1), np.arange(M - 1, HALF, -1)])
    turned = np.zeros((M, M), np.float32)
    turned[np.arange(M), order] = 1.0
    high = lax.Precision.HIGHEST
    pats = jnp.einsum("jk,skl->sjl", turned, pats, precision=high)
    pats = jnp.einsum("sjk,lk->sjl", pats, turned, precision=high)

    def step(x, *grads):
        return x - OBJECT_RATE * sum(grads[1:], grads[0])

    probe = tile_block(probe, 0, 0)
    own00, own01 = tile_block(object_slab, 0, 0), tile_block(object_slab, 0, 1)
    own10, own11 = tile_block(object_slab, 1, 0), tile_block(object_slab, 1, 1)
    own20, own21 = shift(own00, "row", -1), shift(own01, "row", -1)
    own02, own12 = shift(own00, COL, -1), shift(own10, COL, -1)
    own22 = shift(own20, COL, -1)

    blocks = (own00, own01, own02, own10, own11, own12, own20, own21, own22)
    g00, g01, g02, g10, g11, g12, g20, g21, g22, gprobe = windows(offs, count, blocks, probe, pats, tables)
    terms = deal(gprobe)
    left0, left2 = shift(g02, COL, 1), shift(g22, COL, 1)
    above1, under1 = shift(g21, "row", 1), shift(g01, "row", -1)
    left1 = shift(g12, COL, 1)
    g00, g20 = together(g00 + left0, g20 + left2)
    summed = collect(together(terms, g00, g20)[0], probe.shape)
    own10 = step(own10, g10, left1)
    above0, under0, own12, own01, own11, own21 = together(
        shift(g20, "row", 1), shift(g00, "row", -1), shift(own10, COL, -1),
        step(own01, g01, above1), step(own11, g11), step(own21, g21, under1),
    )
    own00, own20 = together(step(own00, g00, above0), step(own20, g20, under0))
    own02, own22 = shift(own00, COL, -1), shift(own20, COL, -1)
    probe = probe - pstep * summed

    blocks = (own00, own01, own02, own10, own11, own12, own20, own21, own22)
    g00, g01, g02, g10, g11, g12, g20, g21, g22, gprobe = windows(offs, count, blocks, probe, pats, tables)
    terms = deal(gprobe)
    left2, left0, left1 = shift(g22, COL, 1), shift(g02, COL, 1), shift(g12, COL, 1)
    above1 = shift_z(g21, 1)
    g20 = g20 + left2
    above0, (far1, wrapped) = shift(g20, "row", 1), cross_y(above1, 1)
    summed = collect(together(terms, g20)[0], probe.shape)
    whole = most((own00, own01, own10, own11), (g00, g01, g10, g11, left0, left1))
    above0, far1, summed, whole = together(above0, far1, summed, whole)
    return rest(pstep, wrapped, (above0, above1, far1), probe, summed, whole)


def solution(mesh):
    mesh = Mesh(mesh.devices.reshape(-1, 4, 2, 2), ("row", *COL))
    placed = (
        P(None, "row", COL),
        P(),
        P("row", COL, None, None),
        P("row", COL),
        P("row", COL, None, None, None),
    )
    return jax.shard_map(
        body, mesh=mesh, in_specs=placed, out_specs=(P(None, "row", COL), P()), check_vma=False
    )
```

```python
import functools
import itertools
import math

import jax
import jax.numpy as jnp
import numpy as np
from jax import lax
from jax.experimental import pallas as pl
from jax.experimental.pallas import tpu as pltpu
from jax.sharding import Mesh, PartitionSpec as P

OBJECT_RATE = 0.1
PROBE_RATE = 0.5
M = 256
HALF = M // 2
LANES = 128
COL = ("x", "y_lo", "core")
STRIP = 32
F32 = jnp.float32
BF16 = jnp.bfloat16


def packed_tables():
    j = np.arange(HALF)[:, None]
    k = np.arange(M)[None, :]
    angle = 2.0 * np.pi * ((j * k) % M) / M
    cosine = np.cos(angle)
    sine = np.sin(angle)
    sine[0] = np.where(np.arange(M) % 2 == 0, 1.0, -1.0)
    table = np.concatenate([cosine, sine]) / math.sqrt(M)

    def split(t):
        high = t.astype(jnp.bfloat16)
        low = (t - high.astype(np.float64)).astype(jnp.bfloat16)
        return high, low

    return split(table) + split(table.T)


def split_parts(x):
    high = x.astype(BF16)
    low = (x - high.astype(F32)).astype(BF16)
    return high, low

def butterfly(uc, us, vc, vs, first):
    if first is None:
        return uc + vs, uc - vs, vc - us, vc + us
    rp = uc + jnp.where(first, 0.0, vs)
    rm = jnp.where(first, us, uc - vs)
    ip = vc - jnp.where(first, 0.0, us)
    im = jnp.where(first, vs, vc + us)
    return rp, rm, ip, im

def butterfly_adjoint(rp, rm, ip, im, first):
    if first is None:
        return rp + rm, im - ip, ip + im, rp - rm
    uc = rp + jnp.where(first, 0.0, rm)
    vs = jnp.where(first, im, rp - rm)
    vc = ip + jnp.where(first, 0.0, im)
    us = jnp.where(first, rm, im - ip)
    return uc, us, vc, vs

def halves(x):
    return x[:, :LANES], x[:, LANES:]

def window(s, live, offs, probe, pats, tables, ext, gacc, pacc, scratch):
    rh, rl, th, tl = tables
    ah, al, bh, bl, f, pr = scratch
    r = offs[0, s]
    c = offs[1, s]
    a = c // LANES
    b = c - a * LANES
    lane = lax.broadcasted_iota(jnp.int32, (STRIP, LANES), 1)
    keep = lane >= b
    lane_first = lane == 0
    row_first = lax.broadcasted_iota(jnp.int32, (STRIP, M), 0) == 0

    def cut(part, i):
        rows = pl.ds(r + i * STRIP, STRIP)
        t0 = ext[a, part, rows, :]
        t1 = ext[a + 1, part, rows, :]
        t2 = ext[a + 2, part, rows, :]
        return jnp.concatenate([jnp.where(keep, t0, t2), t1], axis=1)

    def turn(part, i):
        rows = pl.ds(i * STRIP, STRIP)
        p0 = pltpu.roll(probe[0, part, rows, :], b, 1)
        p1 = pltpu.roll(probe[1, part, rows, :], b, 1)
        return jnp.concatenate([jnp.where(keep, p0, p1), jnp.where(keep, p1, p0)], axis=1)

    def put(high, low, part, rows, value):
        h, l = split_parts(value)
        high[part, rows, :] = h
        low[part, rows, :] = l

    def right(high, low, wh, wl, emit):
        w = jnp.concatenate([wh[...], wh[...], wl[...]], axis=0)
        for part in range(2):
            h, l = high[part], low[part]
            emit(part, slice(0, M), jnp.dot(jnp.concatenate([h, l, h], axis=1), w, preferred_element_type=F32))

    def left(wh, wl, high, low, emit):
        w = jnp.concatenate([wh[...], wl[...], wh[...]], axis=1)
        for part in range(2):
            h, l = high[part], low[part]
            x = jnp.concatenate([h, h, l], axis=0)
            emit(part, slice(0, M), jnp.dot(w, x, preferred_element_type=F32))

    def keep_f32(part, rows, value):
        f[part, rows, :] = value

    for i in range(M // STRIP):
        rows = slice(i * STRIP, (i + 1) * STRIP)
        o_re, o_im = cut(0, i), cut(1, i)
        p_re, p_im = turn(0, i), turn(1, i)
        pr[0, rows, :] = p_re
        pr[1, rows, :] = p_im
        put(ah, al, 0, rows, p_re * o_re - p_im * o_im)
        put(ah, al, 1, rows, p_re * o_im + p_im * o_re)
    yield
    right(ah, al, th, tl, functools.partial(put, bh, bl))
    yield
    left(rh, rl, bh, bl, keep_f32)
    yield
    for i in range(HALF // STRIP):
        top = slice(i * STRIP, (i + 1) * STRIP)
        bot = slice(HALF + i * STRIP, HALF + (i + 1) * STRIP)
        first = row_first if i == 0 else None
        u_c, u_s, v_c, v_s = f[0, top, :], f[0, bot, :], f[1, top, :], f[1, bot, :]
        wide = []
        for u, v in ((u_c, v_c), (u_s, v_s)):
            rp, rm, ip, im = butterfly(*halves(u), *halves(v), lane_first)
            wide += [jnp.concatenate([rp, rm], axis=1), jnp.concatenate([ip, im], axis=1)]
        rp, rm, ip, im = butterfly(wide[0], wide[2], wide[1], wide[3], first)
        res_p = rp * rp + ip * ip - pats[s, top, :]
        res_m = rm * rm + im * im - pats[s, bot, :]
        if live is not None:
            res_p, res_m = res_p * live, res_m * live
        uc, us, vc, vs = butterfly_adjoint(res_p * rp, res_m * rm, res_p * ip, res_m * im, first)
        for u, v, rows in ((uc, vc, top), (us, vs, bot)):
            x_c, x_s, y_c, y_s = butterfly_adjoint(*halves(u), *halves(v), lane_first)
            put(ah, al, 0, rows, jnp.concatenate([x_c, x_s], axis=1))
            put(ah, al, 1, rows, jnp.concatenate([y_c, y_s], axis=1))
    yield
    left(th, tl, ah, al, functools.partial(put, bh, bl))
    yield
    right(bh, bl, rh, rl, keep_f32)
    yield
    back = lane < LANES - b
    for i in range(M // STRIP):
        rows = slice(i * STRIP, (i + 1) * STRIP)
        spot = pl.ds(r + i * STRIP, STRIP)
        b_re, b_im = f[0, rows, :], f[1, rows, :]
        o_re, o_im = cut(0, i), cut(1, i)
        p_re, p_im = pr[0, rows, :], pr[1, rows, :]
        go = (p_re * b_re + p_im * b_im, p_re * b_im - p_im * b_re)
        gp = (o_re * b_re + o_im * b_im, o_re * b_im - o_im * b_re)
        for part in range(2):
            g0, g1 = halves(go[part])
            gacc[a, part, spot, :] += jnp.where(keep, g0, 0.0)
            gacc[a + 1, part, spot, :] += g1
            gacc[a + 2, part, spot, :] += jnp.where(keep, 0.0, g0)
            q0, q1 = halves(gp[part])
            q0 = pltpu.roll(q0, LANES - b, 1)
            q1 = pltpu.roll(q1, LANES - b, 1)
            pacc[0, part, rows, :] += jnp.where(back, q0, q1)
            pacc[1, part, rows, :] += jnp.where(back, q1, q0)


def windows_kernel(*refs):
    offs, count = refs[:2]
    blocks, (probe, pats) = refs[2:11], refs[11:13]
    tables, grads, gprobe_out = refs[13:17], refs[17:26], refs[26]
    ext, gacc, pats_here, probe_here, gprobe, *scratch = refs[27:]
    *scratch, table0, table1, table2, table3, sem_in, sem_out = scratch
    tables_here = (table0, table1, table2, table3)

    def place(buffer, k):
        i, j = divmod(k, 3)
        return buffer.at[2 * j:2 * j + 2, :, i * M:(i + 1) * M, :]

    arrivals = [pltpu.make_async_copy(blocks[k], place(ext, k), sem_in.at[k]) for k in range(9)]
    others = ((pats, pats_here), (probe, probe_here), *zip(tables, tables_here))
    arrivals += [pltpu.make_async_copy(there, here, sem_in.at[9 + k]) for k, (there, here) in enumerate(others)]
    for copy in arrivals:
        copy.start()

    def clear(i, carry):
        gacc[:, :, pl.ds(i * STRIP, STRIP), :] = jnp.zeros((6, 2, STRIP, LANES), F32)
        return carry

    lax.fori_loop(0, 3 * M // STRIP, clear, 0)
    gprobe[...] = jnp.zeros(gprobe.shape, F32)
    for copy in arrivals:
        copy.wait()

    def pair(k, carry):
        turns = []
        for n in range(4):
            live = None if n == 0 else jnp.where(4 * k + n < count[0], 1.0, 0.0)
            own = [buffer.at[n] for buffer in scratch]
            turns.append(window(4 * k + n, live, offs, probe_here, pats_here, tables_here, ext, gacc, gprobe, own))
        for _ in itertools.zip_longest(*turns):
            pass
        return carry

    lax.fori_loop(0, (count[0] + 3) // 4, pair, 0)
    departures = [pltpu.make_async_copy(place(gacc, k), grads[k], sem_out.at[k]) for k in range(9)]
    departures.append(pltpu.make_async_copy(gprobe, gprobe_out, sem_out.at[9]))
    for copy in departures:
        copy.start()
    for copy in departures:
        copy.wait()


def in_hbm(arrays):
    return [pltpu.with_memory_space_constraint(x, pltpu.HBM) for x in arrays]


def windows(offs, count, blocks, probe, pats, tables):
    smem = pl.BlockSpec(memory_space=pltpu.SMEM)
    where = pl.BlockSpec(memory_space=pl.ANY)
    block = jax.ShapeDtypeStruct((2, 2, M, LANES), F32)
    halves16 = pltpu.VMEM((4, 2, M, M), BF16)
    whole32 = pltpu.VMEM((4, 2, M, M), F32)
    extended = pltpu.VMEM((6, 2, 3 * M, LANES), F32)
    return pl.pallas_call(
        windows_kernel,
        out_shape=[pltpu.HBM(block.shape, F32)] * 10,
        in_specs=[smem, smem] + [where] * 15,
        out_specs=[where] * 10,
        scratch_shapes=[extended, extended] + [pltpu.VMEM(x.shape, F32) for x in (pats, probe, block)]
        + [halves16] * 4 + [whole32] * 2 + [pltpu.VMEM(tables[0].shape, BF16)] * 4
        + [pltpu.SemaphoreType.DMA((15,)), pltpu.SemaphoreType.DMA((10,))],
        compiler_params=pltpu.CompilerParams(vmem_limit_bytes=34 * 1024 * 1024),
        name="windows",
    )(offs, count, *in_hbm([*blocks, probe, pats]), *tables)


def shift(block, axis, distance):
    n = lax.axis_size(axis)
    return lax.ppermute(block, axis, [(i, (i + distance) % n) for i in range(n)])


RING = 4


def shift_z(block, distance):
    pairs = [(i, i // RING * RING + (i + distance) % RING) for i in range(lax.axis_size("row"))]
    return lax.ppermute(block, "row", pairs)


def cross_y(block, distance):
    n, edge = lax.axis_size("row"), 0 if distance > 0 else RING - 1
    wrapped = (lax.axis_index("row") % RING == edge).astype(jnp.int32).reshape(1)
    return lax.ppermute(block, "row", [(i, (i + RING) % n) for i in range(edge, n, RING)]), wrapped


def fetch(refs, here, sem):
    copies = [pltpu.make_async_copy(ref, here.at[k], sem.at[k]) for k, ref in enumerate(refs)]
    for copy in copies:
        copy.start()
    for copy in copies:
        copy.wait()


def most_kernel(*refs):
    whole, here, sem = refs[10:]
    fetch(refs[:10], here, sem)
    for k, grads in enumerate(((4, 8), (5,), (6, 9), (7,))):
        i, j = divmod(k, 2)
        for tile in range(2):
            lanes = pl.ds((2 * j + tile) * LANES, LANES)
            for part in range(2):
                total = sum((here[g, tile, part] for g in grads[1:]), here[grads[0], tile, part])
                whole[part, pl.ds(i * M, M), lanes] = here[k, tile, part] - OBJECT_RATE * total


def rest_kernel(wrapped, above0, near, far, whole_in, whole, top, here, sem, sem_top):
    del whole_in
    view = whole.at[:, pl.ds(0, M), :]
    arrive = pltpu.make_async_copy(view, top, sem_top.at[0])
    arrive.start()
    fetch((above0, near, far), here, sem)
    arrive.wait()
    from_far = wrapped[0] == 1
    for tile in range(2):
        for part in range(2):
            lanes, beside = pl.ds(tile * LANES, LANES), pl.ds((2 + tile) * LANES, LANES)
            top[part, :, lanes] = top[part, :, lanes] - OBJECT_RATE * here[0, tile, part]
            above1 = jnp.where(from_far, here[2, tile, part], here[1, tile, part])
            top[part, :, beside] = top[part, :, beside] - OBJECT_RATE * above1
    leave = pltpu.make_async_copy(top, view, sem_top.at[1])
    leave.start()
    leave.wait()


def probe_kernel(pstep, probe, summed, out):
    for tile in range(2):
        for part in range(2):
            out[part, :, tile * LANES:(tile + 1) * LANES] = probe[tile, part] - pstep * summed[tile, part]


def most(own, grads):
    vmem, where = pl.BlockSpec(memory_space=pltpu.VMEM), pl.BlockSpec(memory_space=pl.ANY)
    return pl.pallas_call(
        most_kernel,
        out_shape=jax.ShapeDtypeStruct((2, 2 * M, 2 * M), F32),
        in_specs=[where] * 10,
        out_specs=vmem,
        scratch_shapes=[pltpu.VMEM((10, *own[0].shape), F32), pltpu.SemaphoreType.DMA((10,))],
        compiler_params=pltpu.CompilerParams(vmem_limit_bytes=24 * 1024 * 1024),
        name="most",
    )(*in_hbm([*own, *grads]))


def rest(wrapped, moved, whole):
    where = pl.BlockSpec(memory_space=pl.ANY)
    return pl.pallas_call(
        rest_kernel,
        out_shape=pltpu.HBM(whole.shape, F32),
        in_specs=[pl.BlockSpec(memory_space=pltpu.SMEM)] + [where] * 4,
        out_specs=where,
        scratch_shapes=[
            pltpu.VMEM((2, M, 2 * M), F32),
            pltpu.VMEM((3, *moved[0].shape), F32),
            pltpu.SemaphoreType.DMA((3,)),
            pltpu.SemaphoreType.DMA((2,)),
        ],
        input_output_aliases={4: 0},
        compiler_params=pltpu.CompilerParams(vmem_limit_bytes=24 * 1024 * 1024),
        name="rest",
    )(wrapped, *in_hbm([*moved, whole]))


def last_probe(pstep, probe, summed):
    vmem = pl.BlockSpec(memory_space=pltpu.VMEM)
    return pl.pallas_call(
        functools.partial(probe_kernel, pstep),
        out_shape=jax.ShapeDtypeStruct((2, M, M), F32),
        in_specs=[vmem] * 2,
        out_specs=vmem,
        compiler_params=pltpu.CompilerParams(vmem_limit_bytes=24 * 1024 * 1024),
        name="last_probe",
    )(probe, summed)


def deal(x):
    return lax.all_to_all(x.reshape(-1, 8, LANES), ("row", *COL), 0, 0, tiled=True)


def collect(terms, shape):
    spread = jnp.broadcast_to(jnp.sum(terms, axis=0)[None], terms.shape)
    return lax.all_to_all(spread, ("row", *COL), 0, 0, tiled=True).reshape(shape)


def together(*values):
    return lax.optimization_barrier(values)


def tile_block(x, i, j):
    part = x[:, i * M:(i + 1) * M, j * M:(j + 1) * M]
    return jnp.stack([part[:, :, :LANES], part[:, :, LANES:]])


def body(object_slab, probe, offsets, counts, patterns):
    tile_h, tile_w = object_slab.shape[1:]
    slots = patterns.shape[2]
    offs = offsets[0, 0]
    count = counts[0]
    tables = tuple(jnp.asarray(t) for t in packed_tables())
    axes = ("row", *COL)
    pstep = PROBE_RATE / math.sqrt(lax.axis_size(axes) * slots)

    pats = patterns[0, 0]
    order = np.concatenate([np.arange(HALF + 1), np.arange(M - 1, HALF, -1)])
    turned = np.zeros((M, M), np.float32)
    turned[np.arange(M), order] = 1.0
    high = lax.Precision.HIGHEST
    pats = jnp.einsum("jk,skl->sjl", turned, pats, precision=high)
    pats = jnp.einsum("sjk,lk->sjl", pats, turned, precision=high)

    def step(x, *grads):
        return x - OBJECT_RATE * sum(grads[1:], grads[0])

    probe = tile_block(probe, 0, 0)
    own00, own01 = tile_block(object_slab, 0, 0), tile_block(object_slab, 0, 1)
    own10, own11 = tile_block(object_slab, 1, 0), tile_block(object_slab, 1, 1)
    own20, own21 = shift(own00, "row", -1), shift(own01, "row", -1)
    own02, own12 = shift(own00, COL, -1), shift(own10, COL, -1)
    own22 = shift(own20, COL, -1)

    blocks = (own00, own01, own02, own10, own11, own12, own20, own21, own22)
    g00, g01, g02, g10, g11, g12, g20, g21, g22, gprobe = windows(offs, count, blocks, probe, pats, tables)
    terms = deal(gprobe)
    left0, left2 = shift(g02, COL, 1), shift(g22, COL, 1)
    above1, under1 = shift(g21, "row", 1), shift(g01, "row", -1)
    left1 = shift(g12, COL, 1)
    g00, g20 = together(g00 + left0, g20 + left2)
    summed = collect(together(terms, g00, g20)[0], probe.shape)
    own10 = step(own10, g10, left1)
    above0, under0, own12, own01, own11, own21 = together(
        shift(g20, "row", 1), shift(g00, "row", -1), shift(own10, COL, -1),
        step(own01, g01, above1), step(own11, g11), step(own21, g21, under1),
    )
    own00, own20 = together(step(own00, g00, above0), step(own20, g20, under0))
    own02, own22 = shift(own00, COL, -1), shift(own20, COL, -1)
    probe = probe - pstep * summed

    blocks = (own00, own01, own02, own10, own11, own12, own20, own21, own22)
    g00, g01, g02, g10, g11, g12, g20, g21, g22, gprobe = windows(offs, count, blocks, probe, pats, tables)
    terms = deal(gprobe)
    left2, left0, left1 = shift(g22, COL, 1), shift(g02, COL, 1), shift(g12, COL, 1)
    above1 = shift_z(g21, 1)
    g20 = g20 + left2
    above0, (far1, wrapped) = shift(g20, "row", 1), cross_y(above1, 1)
    summed = collect(together(terms, g20)[0], probe.shape)
    whole = most((own00, own01, own10, own11), (g00, g01, g10, g11, left0, left1))
    whole = rest(wrapped, (above0, above1, far1), whole)
    summed, whole = together(summed, whole)
    return whole, last_probe(pstep, probe, summed)


def solution(mesh):
    mesh = Mesh(mesh.devices.reshape(-1, 4, 2, 2), ("row", *COL))
    placed = (
        P(None, "row", COL),
        P(),
        P("row", COL, None, None),
        P("row", COL),
        P("row", COL, None, None, None),
    )
    return jax.shard_map(
        body, mesh=mesh, in_specs=placed, out_specs=(P(None, "row", COL), P()), check_vma=False
    )
```

```python
import functools
import itertools
import math

import jax
import jax.numpy as jnp
import numpy as np
from jax import lax
from jax.experimental import pallas as pl
from jax.experimental.pallas import tpu as pltpu
from jax.sharding import Mesh, PartitionSpec as P

OBJECT_RATE = 0.1
PROBE_RATE = 0.5
M = 256
HALF = M // 2
LANES = 128
COL = ("x", "y_lo", "core")
STRIP = 32
F32 = jnp.float32
BF16 = jnp.bfloat16


def packed_tables():
    j = np.arange(HALF)[:, None]
    k = np.arange(M)[None, :]
    angle = 2.0 * np.pi * ((j * k) % M) / M
    cosine = np.cos(angle)
    sine = np.sin(angle)
    sine[0] = np.where(np.arange(M) % 2 == 0, 1.0, -1.0)
    table = np.concatenate([cosine, sine]) / math.sqrt(M)

    def split(t):
        high = t.astype(jnp.bfloat16)
        low = (t - high.astype(np.float64)).astype(jnp.bfloat16)
        return high, low

    return split(table) + split(table.T)


def split_parts(x):
    high = x.astype(BF16)
    low = (x - high.astype(F32)).astype(BF16)
    return high, low

def butterfly(uc, us, vc, vs, first):
    if first is None:
        return uc + vs, uc - vs, vc - us, vc + us
    rp = uc + jnp.where(first, 0.0, vs)
    rm = jnp.where(first, us, uc - vs)
    ip = vc - jnp.where(first, 0.0, us)
    im = jnp.where(first, vs, vc + us)
    return rp, rm, ip, im

def butterfly_adjoint(rp, rm, ip, im, first):
    if first is None:
        return rp + rm, im - ip, ip + im, rp - rm
    uc = rp + jnp.where(first, 0.0, rm)
    vs = jnp.where(first, im, rp - rm)
    vc = ip + jnp.where(first, 0.0, im)
    us = jnp.where(first, rm, im - ip)
    return uc, us, vc, vs

def halves(x):
    return x[:, :LANES], x[:, LANES:]

def window(s, live, offs, probe, pats, tables, ext, gacc, pacc, scratch):
    rh, rl, th, tl = tables
    ah, al, bh, bl, f, pr = scratch
    r = offs[0, s]
    c = offs[1, s]
    a = c // LANES
    b = c - a * LANES
    lane = lax.broadcasted_iota(jnp.int32, (STRIP, LANES), 1)
    keep = lane >= b
    lane_first = lane == 0
    row_first = lax.broadcasted_iota(jnp.int32, (STRIP, M), 0) == 0

    def cut(part, i):
        rows = pl.ds(r + i * STRIP, STRIP)
        t0 = ext[a, part, rows, :]
        t1 = ext[a + 1, part, rows, :]
        t2 = ext[a + 2, part, rows, :]
        return jnp.concatenate([jnp.where(keep, t0, t2), t1], axis=1)

    def turn(part, i):
        rows = pl.ds(i * STRIP, STRIP)
        p0 = pltpu.roll(probe[0, part, rows, :], b, 1)
        p1 = pltpu.roll(probe[1, part, rows, :], b, 1)
        return jnp.concatenate([jnp.where(keep, p0, p1), jnp.where(keep, p1, p0)], axis=1)

    def put(high, low, part, rows, value):
        h, l = split_parts(value)
        high[part, rows, :] = h
        low[part, rows, :] = l

    def right(high, low, wh, wl, emit):
        w = jnp.concatenate([wh[...], wh[...], wl[...]], axis=0)
        for part in range(2):
            h, l = high[part], low[part]
            emit(part, slice(0, M), jnp.dot(jnp.concatenate([h, l, h], axis=1), w, preferred_element_type=F32))

    def left(wh, wl, high, low, emit):
        w = jnp.concatenate([wh[...], wl[...], wh[...]], axis=1)
        for part in range(2):
            h, l = high[part], low[part]
            x = jnp.concatenate([h, h, l], axis=0)
            emit(part, slice(0, M), jnp.dot(w, x, preferred_element_type=F32))

    def keep_f32(part, rows, value):
        f[part, rows, :] = value

    for i in range(M // STRIP):
        rows = slice(i * STRIP, (i + 1) * STRIP)
        o_re, o_im = cut(0, i), cut(1, i)
        p_re, p_im = turn(0, i), turn(1, i)
        pr[0, rows, :] = p_re
        pr[1, rows, :] = p_im
        put(ah, al, 0, rows, p_re * o_re - p_im * o_im)
        put(ah, al, 1, rows, p_re * o_im + p_im * o_re)
    yield
    right(ah, al, th, tl, functools.partial(put, bh, bl))
    yield
    left(rh, rl, bh, bl, keep_f32)
    yield
    for i in range(HALF // STRIP):
        top = slice(i * STRIP, (i + 1) * STRIP)
        bot = slice(HALF + i * STRIP, HALF + (i + 1) * STRIP)
        first = row_first if i == 0 else None
        u_c, u_s, v_c, v_s = f[0, top, :], f[0, bot, :], f[1, top, :], f[1, bot, :]
        wide = []
        for u, v in ((u_c, v_c), (u_s, v_s)):
            rp, rm, ip, im = butterfly(*halves(u), *halves(v), lane_first)
            wide += [jnp.concatenate([rp, rm], axis=1), jnp.concatenate([ip, im], axis=1)]
        rp, rm, ip, im = butterfly(wide[0], wide[2], wide[1], wide[3], first)
        res_p = rp * rp + ip * ip - pats[s, top, :]
        res_m = rm * rm + im * im - pats[s, bot, :]
        if live is not None:
            res_p, res_m = res_p * live, res_m * live
        uc, us, vc, vs = butterfly_adjoint(res_p * rp, res_m * rm, res_p * ip, res_m * im, first)
        for u, v, rows in ((uc, vc, top), (us, vs, bot)):
            x_c, x_s, y_c, y_s = butterfly_adjoint(*halves(u), *halves(v), lane_first)
            put(ah, al, 0, rows, jnp.concatenate([x_c, x_s], axis=1))
            put(ah, al, 1, rows, jnp.concatenate([y_c, y_s], axis=1))
    yield
    left(th, tl, ah, al, functools.partial(put, bh, bl))
    yield
    right(bh, bl, rh, rl, keep_f32)
    yield
    back = lane < LANES - b
    for i in range(M // STRIP):
        rows = slice(i * STRIP, (i + 1) * STRIP)
        spot = pl.ds(r + i * STRIP, STRIP)
        b_re, b_im = f[0, rows, :], f[1, rows, :]
        o_re, o_im = cut(0, i), cut(1, i)
        p_re, p_im = pr[0, rows, :], pr[1, rows, :]
        go = (p_re * b_re + p_im * b_im, p_re * b_im - p_im * b_re)
        gp = (o_re * b_re + o_im * b_im, o_re * b_im - o_im * b_re)
        for part in range(2):
            g0, g1 = halves(go[part])
            gacc[a, part, spot, :] += jnp.where(keep, g0, 0.0)
            gacc[a + 1, part, spot, :] += g1
            gacc[a + 2, part, spot, :] += jnp.where(keep, 0.0, g0)
            q0, q1 = halves(gp[part])
            q0 = pltpu.roll(q0, LANES - b, 1)
            q1 = pltpu.roll(q1, LANES - b, 1)
            pacc[0, part, rows, :] += jnp.where(back, q0, q1)
            pacc[1, part, rows, :] += jnp.where(back, q1, q0)


def windows_kernel(*refs):
    offs, count = refs[:2]
    blocks, (probe, pats) = refs[2:11], refs[11:13]
    tables, grads, gprobe_out = refs[13:17], refs[17:26], refs[26]
    ext, gacc, pats_here, probe_here, gprobe, *scratch = refs[27:]
    *scratch, table0, table1, table2, table3, sem_in, sem_out = scratch
    tables_here = (table0, table1, table2, table3)

    def place(buffer, k):
        i, j = divmod(k, 3)
        return buffer.at[2 * j:2 * j + 2, :, i * M:(i + 1) * M, :]

    arrivals = [pltpu.make_async_copy(blocks[k], place(ext, k), sem_in.at[k]) for k in range(9)]
    others = ((pats, pats_here), (probe, probe_here), *zip(tables, tables_here))
    arrivals += [pltpu.make_async_copy(there, here, sem_in.at[9 + k]) for k, (there, here) in enumerate(others)]
    for copy in arrivals:
        copy.start()

    def clear(i, carry):
        gacc[:, :, pl.ds(i * STRIP, STRIP), :] = jnp.zeros((6, 2, STRIP, LANES), F32)
        return carry

    lax.fori_loop(0, 3 * M // STRIP, clear, 0)
    gprobe[...] = jnp.zeros(gprobe.shape, F32)
    for copy in arrivals:
        copy.wait()

    def pair(k, carry):
        turns = []
        for n in range(4):
            live = None if n == 0 else jnp.where(4 * k + n < count[0], 1.0, 0.0)
            own = [buffer.at[n] for buffer in scratch]
            turns.append(window(4 * k + n, live, offs, probe_here, pats_here, tables_here, ext, gacc, gprobe, own))
        for _ in itertools.zip_longest(*turns):
            pass
        return carry

    lax.fori_loop(0, (count[0] + 3) // 4, pair, 0)
    departures = [pltpu.make_async_copy(place(gacc, k), grads[k], sem_out.at[k]) for k in range(9)]
    departures.append(pltpu.make_async_copy(gprobe, gprobe_out, sem_out.at[9]))
    for copy in departures:
        copy.start()
    for copy in departures:
        copy.wait()


def in_hbm(arrays):
    return [pltpu.with_memory_space_constraint(x, pltpu.HBM) for x in arrays]


def windows(offs, count, blocks, probe, pats, tables):
    smem = pl.BlockSpec(memory_space=pltpu.SMEM)
    where = pl.BlockSpec(memory_space=pl.ANY)
    block = jax.ShapeDtypeStruct((2, 2, M, LANES), F32)
    halves16 = pltpu.VMEM((4, 2, M, M), BF16)
    whole32 = pltpu.VMEM((4, 2, M, M), F32)
    extended = pltpu.VMEM((6, 2, 3 * M, LANES), F32)
    return pl.pallas_call(
        windows_kernel,
        out_shape=[pltpu.HBM(block.shape, F32)] * 10,
        in_specs=[smem, smem] + [where] * 15,
        out_specs=[where] * 10,
        scratch_shapes=[extended, extended] + [pltpu.VMEM(x.shape, F32) for x in (pats, probe, block)]
        + [halves16] * 4 + [whole32] * 2 + [pltpu.VMEM(tables[0].shape, BF16)] * 4
        + [pltpu.SemaphoreType.DMA((15,)), pltpu.SemaphoreType.DMA((10,))],
        compiler_params=pltpu.CompilerParams(vmem_limit_bytes=34 * 1024 * 1024),
        name="windows",
    )(offs, count, *in_hbm([*blocks, probe, pats]), *tables)


def shift(block, axis, distance):
    n = lax.axis_size(axis)
    return lax.ppermute(block, axis, [(i, (i + distance) % n) for i in range(n)])


RING = 4


def shift_z(block, distance):
    pairs = [(i, i // RING * RING + (i + distance) % RING) for i in range(lax.axis_size("row"))]
    return lax.ppermute(block, "row", pairs)


def cross_y(block, distance):
    n, edge = lax.axis_size("row"), 0 if distance > 0 else RING - 1
    wrapped = (lax.axis_index("row") % RING == edge).astype(jnp.int32).reshape(1)
    return lax.ppermute(block, "row", [(i, (i + RING) % n) for i in range(edge, n, RING)]), wrapped


def fetch(refs, here, sem):
    copies = [pltpu.make_async_copy(ref, here.at[k], sem.at[k]) for k, ref in enumerate(refs)]
    for copy in copies:
        copy.start()
    for copy in copies:
        copy.wait()


def most_kernel(*refs):
    whole, here, sem = refs[10:]
    fetch(refs[:10], here, sem)
    for k, grads in enumerate(((4, 8), (5,), (6, 9), (7,))):
        i, j = divmod(k, 2)
        for tile in range(2):
            lanes = pl.ds((2 * j + tile) * LANES, LANES)
            for part in range(2):
                total = sum((here[g, tile, part] for g in grads[1:]), here[grads[0], tile, part])
                whole[part, pl.ds(i * M, M), lanes] = here[k, tile, part] - OBJECT_RATE * total


def rest_kernel(wrapped, above0, near, far, whole_in, whole, top, here, sem, sem_top):
    del whole_in
    view = whole.at[:, pl.ds(0, M), :]
    arrive = pltpu.make_async_copy(view, top, sem_top.at[0])
    arrive.start()
    fetch((above0, near, far), here, sem)
    arrive.wait()
    from_far = wrapped[0] == 1
    for tile in range(2):
        for part in range(2):
            lanes, beside = pl.ds(tile * LANES, LANES), pl.ds((2 + tile) * LANES, LANES)
            top[part, :, lanes] = top[part, :, lanes] - OBJECT_RATE * here[0, tile, part]
            above1 = jnp.where(from_far, here[2, tile, part], here[1, tile, part])
            top[part, :, beside] = top[part, :, beside] - OBJECT_RATE * above1
    leave = pltpu.make_async_copy(top, view, sem_top.at[1])
    leave.start()
    leave.wait()


def probe_kernel(pstep, probe, summed, out):
    for tile in range(2):
        for part in range(2):
            out[part, :, tile * LANES:(tile + 1) * LANES] = probe[tile, part] - pstep * summed[tile, part]


def most(own, grads):
    vmem, where = pl.BlockSpec(memory_space=pltpu.VMEM), pl.BlockSpec(memory_space=pl.ANY)
    return pl.pallas_call(
        most_kernel,
        out_shape=jax.ShapeDtypeStruct((2, 2 * M, 2 * M), F32),
        in_specs=[where] * 10,
        out_specs=vmem,
        scratch_shapes=[pltpu.VMEM((10, *own[0].shape), F32), pltpu.SemaphoreType.DMA((10,))],
        compiler_params=pltpu.CompilerParams(vmem_limit_bytes=24 * 1024 * 1024),
        name="most",
    )(*in_hbm([*own, *grads]))


def rest(wrapped, moved, whole):
    where = pl.BlockSpec(memory_space=pl.ANY)
    return pl.pallas_call(
        rest_kernel,
        out_shape=pltpu.HBM(whole.shape, F32),
        in_specs=[pl.BlockSpec(memory_space=pltpu.SMEM)] + [where] * 4,
        out_specs=where,
        scratch_shapes=[
            pltpu.VMEM((2, M, 2 * M), F32),
            pltpu.VMEM((3, *moved[0].shape), F32),
            pltpu.SemaphoreType.DMA((3,)),
            pltpu.SemaphoreType.DMA((2,)),
        ],
        input_output_aliases={4: 0},
        compiler_params=pltpu.CompilerParams(vmem_limit_bytes=24 * 1024 * 1024),
        name="rest",
    )(wrapped, *in_hbm([*moved, whole]))


def last_probe(pstep, probe, summed):
    vmem = pl.BlockSpec(memory_space=pltpu.VMEM)
    return pl.pallas_call(
        functools.partial(probe_kernel, pstep),
        out_shape=jax.ShapeDtypeStruct((2, M, M), F32),
        in_specs=[vmem] * 2,
        out_specs=vmem,
        compiler_params=pltpu.CompilerParams(vmem_limit_bytes=24 * 1024 * 1024),
        name="last_probe",
    )(probe, summed)


def deal(x):
    return lax.all_to_all(x.reshape(-1, 8, LANES), ("row", *COL), 0, 0, tiled=True)


def collect(terms, shape):
    spread = jnp.broadcast_to(jnp.sum(terms, axis=0)[None], terms.shape)
    return lax.all_to_all(spread, ("row", *COL), 0, 0, tiled=True).reshape(shape)


def together(*values):
    return lax.optimization_barrier(values)


def tile_block(x, i, j):
    part = x[:, i * M:(i + 1) * M, j * M:(j + 1) * M]
    return jnp.stack([part[:, :, :LANES], part[:, :, LANES:]])


def body(object_slab, probe, offsets, counts, patterns):
    tile_h, tile_w = object_slab.shape[1:]
    slots = patterns.shape[2]
    offs = offsets[0, 0]
    count = counts[0]
    tables = tuple(jnp.asarray(t) for t in packed_tables())
    axes = ("row", *COL)
    pstep = PROBE_RATE / math.sqrt(lax.axis_size(axes) * slots)

    pats = patterns[0, 0]
    order = np.concatenate([np.arange(HALF + 1), np.arange(M - 1, HALF, -1)])
    turned = np.zeros((M, M), np.float32)
    turned[np.arange(M), order] = 1.0
    high = lax.Precision.HIGHEST
    pats = jnp.einsum("jk,skl->sjl", turned, pats, precision=high)
    pats = jnp.einsum("sjk,lk->sjl", pats, turned, precision=high)

    def step(x, *grads):
        return x - OBJECT_RATE * sum(grads[1:], grads[0])

    probe = tile_block(probe, 0, 0)
    own00, own01 = tile_block(object_slab, 0, 0), tile_block(object_slab, 0, 1)
    own10, own11 = tile_block(object_slab, 1, 0), tile_block(object_slab, 1, 1)
    own20, own21 = shift(own00, "row", -1), shift(own01, "row", -1)
    own02, own12 = shift(own00, COL, -1), shift(own10, COL, -1)
    own22 = shift(own20, COL, -1)

    blocks = (own00, own01, own02, own10, own11, own12, own20, own21, own22)
    g00, g01, g02, g10, g11, g12, g20, g21, g22, gprobe = windows(offs, count, blocks, probe, pats, tables)
    terms = deal(gprobe)
    left0, left2 = shift(g02, COL, 1), shift(g22, COL, 1)
    above1, under1 = shift(g21, "row", 1), shift(g01, "row", -1)
    left1 = shift(g12, COL, 1)
    g00, g20 = together(g00 + left0, g20 + left2)
    summed = collect(together(terms, g00, g20)[0], probe.shape)
    own10 = step(own10, g10, left1)
    own12 = shift(own10, COL, -1)
    above0, under0, own10, own01, own11, own21 = together(
        shift(g20, "row", 1), shift(g00, "row", -1), own10,
        step(own01, g01, above1), step(own11, g11), step(own21, g21, under1),
    )
    own00, own20 = step(own00, g00, above0), step(own20, g20, under0)
    own02, own22 = shift(own00, COL, -1), shift(own20, COL, -1)
    probe = probe - pstep * summed

    blocks = (own00, own01, own02, own10, own11, own12, own20, own21, own22)
    g00, g01, g02, g10, g11, g12, g20, g21, g22, gprobe = windows(offs, count, blocks, probe, pats, tables)
    terms = deal(gprobe)
    left2, left0, left1 = shift(g22, COL, 1), shift(g02, COL, 1), shift(g12, COL, 1)
    above1 = shift_z(g21, 1)
    g20 = g20 + left2
    above0, (far1, wrapped) = shift(g20, "row", 1), cross_y(above1, 1)
    summed = collect(together(terms, g20)[0], probe.shape)
    whole = most((own00, own01, own10, own11), (g00, g01, g10, g11, left0, left1))
    whole = rest(wrapped, (above0, above1, far1), whole)
    summed, whole = together(summed, whole)
    return whole, last_probe(pstep, probe, summed)


def solution(mesh):
    mesh = Mesh(mesh.devices.reshape(-1, 4, 2, 2), ("row", *COL))
    placed = (
        P(None, "row", COL),
        P(),
        P("row", COL, None, None),
        P("row", COL),
        P("row", COL, None, None, None),
    )
    return jax.shard_map(
        body, mesh=mesh, in_specs=placed, out_specs=(P(None, "row", COL), P()), check_vma=False
    )
```

```python
import functools
import itertools
import math

import jax
import jax.numpy as jnp
import numpy as np
from jax import lax
from jax.experimental import pallas as pl
from jax.experimental.pallas import tpu as pltpu
from jax.sharding import Mesh, PartitionSpec as P

OBJECT_RATE = 0.1
PROBE_RATE = 0.5
M = 256
HALF = M // 2
LANES = 128
COL = ("x", "y_lo", "core")
STRIP = 32
F32 = jnp.float32
BF16 = jnp.bfloat16


def packed_tables():
    j = np.arange(HALF)[:, None]
    k = np.arange(M)[None, :]
    angle = 2.0 * np.pi * ((j * k) % M) / M
    cosine = np.cos(angle)
    sine = np.sin(angle)
    sine[0] = np.where(np.arange(M) % 2 == 0, 1.0, -1.0)
    table = np.concatenate([cosine, sine]) / math.sqrt(M)

    def split(t):
        high = t.astype(jnp.bfloat16)
        low = (t - high.astype(np.float64)).astype(jnp.bfloat16)
        return high, low

    return split(table) + split(table.T)


def split_parts(x):
    high = x.astype(BF16)
    low = (x - high.astype(F32)).astype(BF16)
    return high, low

def butterfly(uc, us, vc, vs, first):
    if first is None:
        return uc + vs, uc - vs, vc - us, vc + us
    rp = uc + jnp.where(first, 0.0, vs)
    rm = jnp.where(first, us, uc - vs)
    ip = vc - jnp.where(first, 0.0, us)
    im = jnp.where(first, vs, vc + us)
    return rp, rm, ip, im

def butterfly_adjoint(rp, rm, ip, im, first):
    if first is None:
        return rp + rm, im - ip, ip + im, rp - rm
    uc = rp + jnp.where(first, 0.0, rm)
    vs = jnp.where(first, im, rp - rm)
    vc = ip + jnp.where(first, 0.0, im)
    us = jnp.where(first, rm, im - ip)
    return uc, us, vc, vs

def halves(x):
    return x[:, :LANES], x[:, LANES:]

def window(s, live, offs, probe, pats, tables, ext, gacc, pacc, scratch):
    rh, rl, th, tl = tables
    ah, al, bh, bl, f, pr = scratch
    r = offs[0, s]
    c = offs[1, s]
    a = c // LANES
    b = c - a * LANES
    lane = lax.broadcasted_iota(jnp.int32, (STRIP, LANES), 1)
    keep = lane >= b
    lane_first = lane == 0
    row_first = lax.broadcasted_iota(jnp.int32, (STRIP, M), 0) == 0

    def cut(part, i):
        rows = pl.ds(r + i * STRIP, STRIP)
        t0 = ext[a, part, rows, :]
        t1 = ext[a + 1, part, rows, :]
        t2 = ext[a + 2, part, rows, :]
        return jnp.concatenate([jnp.where(keep, t0, t2), t1], axis=1)

    def turn(part, i):
        rows = pl.ds(i * STRIP, STRIP)
        p0 = pltpu.roll(probe[0, part, rows, :], b, 1)
        p1 = pltpu.roll(probe[1, part, rows, :], b, 1)
        return jnp.concatenate([jnp.where(keep, p0, p1), jnp.where(keep, p1, p0)], axis=1)

    def put(high, low, part, rows, value):
        h, l = split_parts(value)
        high[part, rows, :] = h
        low[part, rows, :] = l

    def right(high, low, wh, wl, emit):
        w = jnp.concatenate([wh[...], wh[...], wl[...]], axis=0)
        for part in range(2):
            h, l = high[part], low[part]
            emit(part, slice(0, M), jnp.dot(jnp.concatenate([h, l, h], axis=1), w, preferred_element_type=F32))

    def left(wh, wl, high, low, emit):
        w = jnp.concatenate([wh[...], wl[...], wh[...]], axis=1)
        for part in range(2):
            h, l = high[part], low[part]
            x = jnp.concatenate([h, h, l], axis=0)
            emit(part, slice(0, M), jnp.dot(w, x, preferred_element_type=F32))

    def keep_f32(part, rows, value):
        f[part, rows, :] = value

    for i in range(M // STRIP):
        rows = slice(i * STRIP, (i + 1) * STRIP)
        o_re, o_im = cut(0, i), cut(1, i)
        p_re, p_im = turn(0, i), turn(1, i)
        pr[0, rows, :] = p_re
        pr[1, rows, :] = p_im
        put(ah, al, 0, rows, p_re * o_re - p_im * o_im)
        put(ah, al, 1, rows, p_re * o_im + p_im * o_re)
    yield
    right(ah, al, th, tl, functools.partial(put, bh, bl))
    yield
    left(rh, rl, bh, bl, keep_f32)
    yield
    for i in range(HALF // STRIP):
        top = slice(i * STRIP, (i + 1) * STRIP)
        bot = slice(HALF + i * STRIP, HALF + (i + 1) * STRIP)
        first = row_first if i == 0 else None
        u_c, u_s, v_c, v_s = f[0, top, :], f[0, bot, :], f[1, top, :], f[1, bot, :]
        wide = []
        for u, v in ((u_c, v_c), (u_s, v_s)):
            rp, rm, ip, im = butterfly(*halves(u), *halves(v), lane_first)
            wide += [jnp.concatenate([rp, rm], axis=1), jnp.concatenate([ip, im], axis=1)]
        rp, rm, ip, im = butterfly(wide[0], wide[2], wide[1], wide[3], first)
        res_p = rp * rp + ip * ip - pats[s, top, :]
        res_m = rm * rm + im * im - pats[s, bot, :]
        if live is not None:
            res_p, res_m = res_p * live, res_m * live
        uc, us, vc, vs = butterfly_adjoint(res_p * rp, res_m * rm, res_p * ip, res_m * im, first)
        for u, v, rows in ((uc, vc, top), (us, vs, bot)):
            x_c, x_s, y_c, y_s = butterfly_adjoint(*halves(u), *halves(v), lane_first)
            put(ah, al, 0, rows, jnp.concatenate([x_c, x_s], axis=1))
            put(ah, al, 1, rows, jnp.concatenate([y_c, y_s], axis=1))
    yield
    left(th, tl, ah, al, functools.partial(put, bh, bl))
    yield
    right(bh, bl, rh, rl, keep_f32)
    yield
    back = lane < LANES - b
    for i in range(M // STRIP):
        rows = slice(i * STRIP, (i + 1) * STRIP)
        spot = pl.ds(r + i * STRIP, STRIP)
        b_re, b_im = f[0, rows, :], f[1, rows, :]
        o_re, o_im = cut(0, i), cut(1, i)
        p_re, p_im = pr[0, rows, :], pr[1, rows, :]
        go = (p_re * b_re + p_im * b_im, p_re * b_im - p_im * b_re)
        gp = (o_re * b_re + o_im * b_im, o_re * b_im - o_im * b_re)
        for part in range(2):
            g0, g1 = halves(go[part])
            gacc[a, part, spot, :] += jnp.where(keep, g0, 0.0)
            gacc[a + 1, part, spot, :] += g1
            gacc[a + 2, part, spot, :] += jnp.where(keep, 0.0, g0)
            q0, q1 = halves(gp[part])
            q0 = pltpu.roll(q0, LANES - b, 1)
            q1 = pltpu.roll(q1, LANES - b, 1)
            pacc[0, part, rows, :] += jnp.where(back, q0, q1)
            pacc[1, part, rows, :] += jnp.where(back, q1, q0)


def windows_kernel(*refs):
    offs, count = refs[:2]
    blocks, (probe, pats) = refs[2:11], refs[11:13]
    tables, grads, gprobe_out = refs[13:17], refs[17:26], refs[26]
    ext, gacc, pats_here, probe_here, gprobe, *scratch = refs[27:]
    *scratch, table0, table1, table2, table3, sem_in, sem_out = scratch
    tables_here = (table0, table1, table2, table3)

    def place(buffer, k):
        i, j = divmod(k, 3)
        return buffer.at[2 * j:2 * j + 2, :, i * M:(i + 1) * M, :]

    arrivals = [pltpu.make_async_copy(blocks[k], place(ext, k), sem_in.at[k]) for k in range(9)]
    others = ((pats, pats_here), (probe, probe_here), *zip(tables, tables_here))
    arrivals += [pltpu.make_async_copy(there, here, sem_in.at[9 + k]) for k, (there, here) in enumerate(others)]
    for copy in arrivals:
        copy.start()

    def clear(i, carry):
        gacc[:, :, pl.ds(i * STRIP, STRIP), :] = jnp.zeros((6, 2, STRIP, LANES), F32)
        return carry

    lax.fori_loop(0, 3 * M // STRIP, clear, 0)
    gprobe[...] = jnp.zeros(gprobe.shape, F32)
    for copy in arrivals:
        copy.wait()

    def pair(k, carry):
        turns = []
        for n in range(4):
            live = None if n == 0 else jnp.where(4 * k + n < count[0], 1.0, 0.0)
            own = [buffer.at[n] for buffer in scratch]
            turns.append(window(4 * k + n, live, offs, probe_here, pats_here, tables_here, ext, gacc, gprobe, own))
        for _ in itertools.zip_longest(*turns):
            pass
        return carry

    lax.fori_loop(0, (count[0] + 3) // 4, pair, 0)
    departures = [pltpu.make_async_copy(place(gacc, k), grads[k], sem_out.at[k]) for k in range(9)]
    departures.append(pltpu.make_async_copy(gprobe, gprobe_out, sem_out.at[9]))
    for copy in departures:
        copy.start()
    for copy in departures:
        copy.wait()


def in_hbm(arrays):
    return [pltpu.with_memory_space_constraint(x, pltpu.HBM) for x in arrays]


def windows(offs, count, blocks, probe, pats, tables):
    smem = pl.BlockSpec(memory_space=pltpu.SMEM)
    where = pl.BlockSpec(memory_space=pl.ANY)
    block = jax.ShapeDtypeStruct((2, 2, M, LANES), F32)
    halves16 = pltpu.VMEM((4, 2, M, M), BF16)
    whole32 = pltpu.VMEM((4, 2, M, M), F32)
    extended = pltpu.VMEM((6, 2, 3 * M, LANES), F32)
    return pl.pallas_call(
        windows_kernel,
        out_shape=[pltpu.HBM(block.shape, F32)] * 10,
        in_specs=[smem, smem] + [where] * 15,
        out_specs=[where] * 10,
        scratch_shapes=[extended, extended] + [pltpu.VMEM(x.shape, F32) for x in (pats, probe, block)]
        + [halves16] * 4 + [whole32] * 2 + [pltpu.VMEM(tables[0].shape, BF16)] * 4
        + [pltpu.SemaphoreType.DMA((15,)), pltpu.SemaphoreType.DMA((10,))],
        compiler_params=pltpu.CompilerParams(vmem_limit_bytes=34 * 1024 * 1024),
        name="windows",
    )(offs, count, *in_hbm([*blocks, probe, pats]), *tables)


def shift(block, axis, distance):
    n = lax.axis_size(axis)
    return lax.ppermute(block, axis, [(i, (i + distance) % n) for i in range(n)])


RING = 4


def shift_z(block, distance):
    pairs = [(i, i // RING * RING + (i + distance) % RING) for i in range(lax.axis_size("row"))]
    return lax.ppermute(block, "row", pairs)


def cross_y(block, distance):
    n, edge = lax.axis_size("row"), 0 if distance > 0 else RING - 1
    wrapped = (lax.axis_index("row") % RING == edge).astype(jnp.int32).reshape(1)
    return lax.ppermute(block, "row", [(i, (i + RING) % n) for i in range(edge, n, RING)]), wrapped


def fetch(refs, here, sem):
    copies = [pltpu.make_async_copy(ref, here.at[k], sem.at[k]) for k, ref in enumerate(refs)]
    for copy in copies:
        copy.start()
    for copy in copies:
        copy.wait()


def most_kernel(*refs):
    whole, here, sem = refs[10:]
    fetch(refs[:10], here, sem)
    for k, grads in enumerate(((4, 8), (5,), (6, 9), (7,))):
        i, j = divmod(k, 2)
        for tile in range(2):
            lanes = pl.ds((2 * j + tile) * LANES, LANES)
            for part in range(2):
                total = sum((here[g, tile, part] for g in grads[1:]), here[grads[0], tile, part])
                whole[part, pl.ds(i * M, M), lanes] = here[k, tile, part] - OBJECT_RATE * total


def rest_kernel(wrapped, above0, near, far, whole_in, whole, top, here, sem, sem_top):
    del whole_in
    view = whole.at[:, pl.ds(0, M), :]
    arrive = pltpu.make_async_copy(view, top, sem_top.at[0])
    arrive.start()
    fetch((above0, near, far), here, sem)
    arrive.wait()
    from_far = wrapped[0] == 1
    for tile in range(2):
        for part in range(2):
            lanes, beside = pl.ds(tile * LANES, LANES), pl.ds((2 + tile) * LANES, LANES)
            top[part, :, lanes] = top[part, :, lanes] - OBJECT_RATE * here[0, tile, part]
            above1 = jnp.where(from_far, here[2, tile, part], here[1, tile, part])
            top[part, :, beside] = top[part, :, beside] - OBJECT_RATE * above1
    leave = pltpu.make_async_copy(top, view, sem_top.at[1])
    leave.start()
    leave.wait()


def probe_kernel(pstep, probe, summed, out):
    for tile in range(2):
        for part in range(2):
            out[part, :, tile * LANES:(tile + 1) * LANES] = probe[tile, part] - pstep * summed[tile, part]


def most(own, grads):
    vmem, where = pl.BlockSpec(memory_space=pltpu.VMEM), pl.BlockSpec(memory_space=pl.ANY)
    return pl.pallas_call(
        most_kernel,
        out_shape=jax.ShapeDtypeStruct((2, 2 * M, 2 * M), F32),
        in_specs=[where] * 10,
        out_specs=vmem,
        scratch_shapes=[pltpu.VMEM((10, *own[0].shape), F32), pltpu.SemaphoreType.DMA((10,))],
        compiler_params=pltpu.CompilerParams(vmem_limit_bytes=24 * 1024 * 1024),
        name="most",
    )(*in_hbm([*own, *grads]))


def rest(wrapped, moved, whole):
    where = pl.BlockSpec(memory_space=pl.ANY)
    return pl.pallas_call(
        rest_kernel,
        out_shape=pltpu.HBM(whole.shape, F32),
        in_specs=[pl.BlockSpec(memory_space=pltpu.SMEM)] + [where] * 4,
        out_specs=where,
        scratch_shapes=[
            pltpu.VMEM((2, M, 2 * M), F32),
            pltpu.VMEM((3, *moved[0].shape), F32),
            pltpu.SemaphoreType.DMA((3,)),
            pltpu.SemaphoreType.DMA((2,)),
        ],
        input_output_aliases={4: 0},
        compiler_params=pltpu.CompilerParams(vmem_limit_bytes=24 * 1024 * 1024),
        name="rest",
    )(wrapped, *in_hbm([*moved, whole]))


def last_probe(pstep, probe, summed):
    vmem = pl.BlockSpec(memory_space=pltpu.VMEM)
    return pl.pallas_call(
        functools.partial(probe_kernel, pstep),
        out_shape=jax.ShapeDtypeStruct((2, M, M), F32),
        in_specs=[vmem] * 2,
        out_specs=vmem,
        compiler_params=pltpu.CompilerParams(vmem_limit_bytes=24 * 1024 * 1024),
        name="last_probe",
    )(probe, summed)


def deal(x):
    return lax.all_to_all(x.reshape(-1, 8, LANES), ("row", *COL), 0, 0, tiled=True)


def collect(terms, shape):
    spread = jnp.broadcast_to(jnp.sum(terms, axis=0)[None], terms.shape)
    return lax.all_to_all(spread, ("row", *COL), 0, 0, tiled=True).reshape(shape)


def together(*values):
    return lax.optimization_barrier(values)


def tile_block(x, i, j):
    part = x[:, i * M:(i + 1) * M, j * M:(j + 1) * M]
    return jnp.stack([part[:, :, :LANES], part[:, :, LANES:]])


def body(object_slab, probe, offsets, counts, patterns):
    tile_h, tile_w = object_slab.shape[1:]
    slots = patterns.shape[2]
    offs = offsets[0, 0]
    count = counts[0]
    tables = tuple(jnp.asarray(t) for t in packed_tables())
    axes = ("row", *COL)
    pstep = PROBE_RATE / math.sqrt(lax.axis_size(axes) * slots)

    pats = patterns[0, 0]
    order = np.concatenate([np.arange(HALF + 1), np.arange(M - 1, HALF, -1)])
    turned = np.zeros((M, M), np.float32)
    turned[np.arange(M), order] = 1.0
    high = lax.Precision.HIGHEST
    pats = jnp.einsum("jk,skl->sjl", turned, pats, precision=high)
    pats = jnp.einsum("sjk,lk->sjl", pats, turned, precision=high)

    def step(x, *grads):
        return x - OBJECT_RATE * sum(grads[1:], grads[0])

    probe = tile_block(probe, 0, 0)
    own00, own01 = tile_block(object_slab, 0, 0), tile_block(object_slab, 0, 1)
    own10, own11 = tile_block(object_slab, 1, 0), tile_block(object_slab, 1, 1)
    own20, own21 = shift(own00, "row", -1), shift(own01, "row", -1)
    own02, own12 = shift(own00, COL, -1), shift(own10, COL, -1)
    own22 = shift(own20, COL, -1)

    blocks = (own00, own01, own02, own10, own11, own12, own20, own21, own22)
    g00, g01, g02, g10, g11, g12, g20, g21, g22, gprobe = windows(offs, count, blocks, probe, pats, tables)
    terms = deal(gprobe)
    left0, left2 = shift(g02, COL, 1), shift(g22, COL, 1)
    above1, under1 = shift(g21, "row", 1), shift(g01, "row", -1)
    left1 = shift(g12, COL, 1)
    g00, g20 = together(g00 + left0, g20 + left2)
    summed = collect(together(terms, g00, g20)[0], probe.shape)
    own10 = step(own10, g10, left1)
    above0, under0, own12, own01, own11, own21 = together(
        shift(g20, "row", 1), shift(g00, "row", -1), shift(own10, COL, -1),
        step(own01, g01, above1), step(own11, g11), step(own21, g21, under1),
    )
    own00, own20 = step(own00, g00, above0), step(own20, g20, under0)
    own02, own22 = shift(own00, COL, -1), shift(own20, COL, -1)
    probe = probe - pstep * summed

    blocks = (own00, own01, own02, own10, own11, own12, own20, own21, own22)
    g00, g01, g02, g10, g11, g12, g20, g21, g22, gprobe = windows(offs, count, blocks, probe, pats, tables)
    terms = deal(gprobe)
    left2, left0, left1 = shift(g22, COL, 1), shift(g02, COL, 1), shift(g12, COL, 1)
    above1 = shift_z(g21, 1)
    g20 = g20 + left2
    above0, (far1, wrapped) = shift(g20, "row", 1), cross_y(above1, 1)
    summed = collect(together(terms, g20)[0], probe.shape)
    whole = most((own00, own01, own10, own11), (g00, g01, g10, g11, left0, left1))
    whole = rest(wrapped, (above0, above1, far1), whole)
    summed, whole = together(summed, whole)
    return whole, last_probe(pstep, probe, summed)


def solution(mesh):
    mesh = Mesh(mesh.devices.reshape(-1, 4, 2, 2), ("row", *COL))
    placed = (
        P(None, "row", COL),
        P(),
        P("row", COL, None, None),
        P("row", COL),
        P("row", COL, None, None, None),
    )
    return jax.shard_map(
        body, mesh=mesh, in_specs=placed, out_specs=(P(None, "row", COL), P()), check_vma=False
    )
```
